32 devices in a mesh: fsdp: 8 (over z, x), tensor: 4 (over y, core).
Axes of the slice: x: 2, y: 2, z: 4, core: 2. Of those that a mesh axis runs over, the one named last changes fastest.
Arguments:
- activations: float32 [8, 197, 768], P('fsdp'), may hold values from -6 to 6
- image_live: int32 [8], P('fsdp'), may hold values 0 or 1
- expert_routes: int32 [8, 197, 2], P('fsdp'), may hold values from 0 to 3, all different within a row; in each aligned block of 197 rows (0 to 196, 197 to 393, ..., all dimensions but the last counted through in order) at most 123 rows name the same one
- attn_gain_one: bfloat16 [768], P('fsdp'), may hold values from 0.5 to 1.5
- qkv_weight_one: bfloat16 [3, 768, 768], P(None, 'fsdp', 'tensor'), may hold values from -0.21875 to 0.21875
- out_weight_one: bfloat16 [768, 768], P('tensor', 'fsdp'), may hold values from -0.625 to 0.625
- first_feedforward_gain: bfloat16 [768], P('fsdp'), may hold values from 0.5 to 1.5
- up_weight_one: bfloat16 [768, 3072], P('fsdp', 'tensor'), may hold values from -0.21875 to 0.21875
- down_weight_one: bfloat16 [3072, 768], P('tensor', 'fsdp'), may hold values from -0.15625 to 0.15625
- attn_gain_two: bfloat16 [768], P('fsdp'), may hold values from 0.5 to 1.5
- qkv_weight_two: bfloat16 [3, 768, 768], P(None, 'fsdp', 'tensor'), may hold values from -0.21875 to 0.21875
- out_weight_two: bfloat16 [768, 768], P('tensor', 'fsdp'), may hold values from -0.625 to 0.625
- moe_gain_two: bfloat16 [768], P('fsdp'), may hold values from 0.5 to 1.5
- router_weight: bfloat16 [768, 4], P('fsdp'), may hold values from -0.15625 to 0.15625
- expert_up: bfloat16 [4, 768, 3072], P(None, 'fsdp', 'tensor'), may hold values from -0.21875 to 0.21875
- expert_down: bfloat16 [4, 3072, 768], P(None, 'tensor', 'fsdp'), may hold values from -0.3125 to 0.3125
- cotangent: float32 [8, 197, 768], P('fsdp'), may hold values from -6 to 6
Outputs:
- result: float32 [8, 197, 768], P('fsdp')
- input_grad: float32 [8, 197, 768], P('fsdp')
- grad_attn_gain_one: float32 [768], P('fsdp')
- grad_qkv_weight_one: float32 [3, 768, 768], P(None, 'fsdp', 'tensor')
- grad_out_weight_one: float32 [768, 768], P('tensor', 'fsdp')
- grad_mlp_gain_one: float32 [768], P('fsdp')
- grad_up_weight_one: float32 [768, 3072], P('fsdp', 'tensor')
- grad_down_weight_one: float32 [3072, 768], P('tensor', 'fsdp')
- grad_attn_gain_two: float32 [768], P('fsdp')
- grad_qkv_weight_two: float32 [3, 768, 768], P(None, 'fsdp', 'tensor')
- grad_out_weight_two: float32 [768, 768], P('tensor', 'fsdp')
- grad_moe_gain_two: float32 [768], P('fsdp')
- grad_router_weight: float32 [768, 4], P('fsdp')
- grad_expert_up: float32 [4, 768, 3072], P(None, 'fsdp', 'tensor')
- grad_expert_down: float32 [4, 3072, 768], P(None, 'tensor', 'fsdp')
The draws below stay inside these ranges and needn't reach their ends.
Inputs may be any that keep to these rules, and one draw needn't show every extreme that they name: `expert_routes`: each token names two different experts; among the 197 tokens of one index of fsdp no expert is named more than 123 times, a bound that some block reaches.
All inputs are finite; a program needn't handle non-finite values. No bound on the sum of `image_live` on one device may be relied on, other than what follows from the above.
Results may differ from the reference program's by a relative error of at most 0.019.
Values may be sent and summed in bfloat16 or wider, within the bound.
No kernel may reach another device: no remote copies, remote signals or barrier semaphores. Data moves between devices by JAX's collectives and lax.ppermute only.
A program may use at most 128 MiB of HBM per device.

```python
import math
import jax
import jax.numpy as jnp
import numpy as np
from jax import lax

D = 768
NH = 12
HD = 64
FF = 3072
E = 4
SEQ = 197
IMG_DEV = 1
TOK_DEV = 197
CAP = 123
IMAGES = 8


def set_ends(entries, own_key, low, largest):
    longest = entries.shape.index(max(entries.shape))
    spots = []
    for shift in (0, 1):
        where = [jax.random.randint(jax.random.fold_in(own_key, axis), (), 0, length) for axis, length in enumerate(entries.shape)]
        where[longest] = (where[longest] + shift) % entries.shape[longest]
        spots.append(tuple(where))
    return entries.at[spots[0]].set(low).at[spots[1]].set(largest)


def levels(stream_key, shape, pieces, low, largest):
    loudness = 1.0
    for dim, parts in pieces:
        heights = jax.random.uniform(jax.random.fold_in(jax.random.fold_in(stream_key, 6), dim), (parts,), jnp.float32, low / len(pieces), largest / len(pieces))
        loudness = loudness * jnp.repeat(jnp.exp(heights), shape[dim] // parts).reshape((-1,) + (1,) * (len(shape) - 1 - dim))
    return loudness


def deal_out(stream_key, own, number, rows, amount, top, reach, slope):
    sequence = jax.random.permutation(stream_key, amount)
    crowded, common = load_shares(amount, rows * top, reach, slope, True), load_shares(amount, rows * top, reach, slope, False)
    places = jnp.arange(amount)

    def named(tallies, rotation):
        used = int((tallies > 0).sum())
        fixed = max(1, used // 4)
        passed = fixed + (places - fixed + rotation * (used - fixed)) % max(1, amount - fixed)
        return jnp.zeros((amount,), jnp.int32).at[sequence[jnp.where(places < fixed, places, passed)]].set(jnp.asarray(tallies, jnp.int32))

    tallies = jnp.where(number % 4 == 0, named(crowded, number // 4), named(common, number - number // 4 - 1))
    mixed = jax.random.permutation(jax.random.fold_in(own, 3), amount)
    giver, sink = mixed[0:amount // 2 * 2:2], mixed[1:amount // 2 * 2:2]
    room = jnp.minimum(tallies[giver] - 1, reach - tallies[sink]) // 2
    room = jnp.where((giver == sequence[0]) | (sink == sequence[0]) | (tallies[sink] == 0), 0, jnp.maximum(room, 0))
    passed = jax.random.randint(jax.random.fold_in(own, 4), (amount // 2,), 0, 1 << 20) % (room + 1)
    tallies = tallies.at[giver].add(-passed).at[sink].add(passed)
    members = jnp.searchsorted(jnp.cumsum(tallies), jnp.arange(rows * top), side="right").astype(jnp.int32)
    listing = members.reshape(top, rows).T
    listing = listing[jax.random.permutation(jax.random.fold_in(own, 1), rows)]
    rotation = jax.random.randint(jax.random.fold_in(own, 2), (rows, 1), 0, top)
    return jnp.take_along_axis(listing, (jnp.arange(top)[None, :] + rotation) % top, axis=1)


def load_shares(count, total, reach, slope, full):
    portions = [(1 << 20) // math.isqrt(grade ** slope) + 1 for grade in range(1, count + 1)]
    largest = reach if full else min(reach, max(-(-total // count), total * portions[0] // sum(portions)))
    least = 1 if total - largest >= count - 1 else 0
    counts, spare = [largest] + [least] * (count - 1), total - largest - least * (count - 1)
    while spare > 0:
        free = [i for i in range(1, count) if counts[i] < largest] or [i for i in range(1, count) if counts[i] < reach]
        whole, remaining = sum([portions[i] for i in free]), spare
        for i in free:
            extra = min(reach - counts[i], max(1, remaining * portions[i] // whole), spare)
            counts[i] = counts[i] + extra
            spare = spare - extra
    return np.array(counts)


def bell_draw(stream_key, extent, scale, bound, split=(), kind=jnp.bfloat16):
    factor_of = levels(stream_key, extent, split, -0.22, 0.18) if split else 1.0
    drawn = jax.random.normal(stream_key, extent, jnp.float32) * scale * factor_of
    return jnp.minimum(jnp.maximum(drawn, -bound), bound).astype(kind)


def setup_inputs(seed: int = 0) -> dict:
    streams_of = jax.random.split(jax.random.key(seed), 18)
    activations = bell_draw(streams_of[0], (IMAGES, SEQ, D), 1.0, 6.0, ((0, 8),), jnp.float32)
    image_live = set_ends((jax.random.randint(streams_of[1], (IMAGES,), 0, 4) < 3).astype(jnp.int32), jax.random.fold_in(streams_of[1], 1), 0, 1)
    expert_routes_keys = jax.random.split(jax.random.fold_in(streams_of[2], 1), IMAGES * SEQ // TOK_DEV)
    expert_routes_turns = jax.random.permutation(jax.random.fold_in(streams_of[2], 3), IMAGES * SEQ // TOK_DEV)
    expert_routes = jax.vmap(lambda own, number: deal_out(jax.random.fold_in(streams_of[2], 2), own, number, TOK_DEV, E, 2, CAP, 1))(expert_routes_keys, expert_routes_turns).reshape((IMAGES, SEQ, 2))
    attn_gain_one = jnp.clip(1.0 + 0.1 * jax.random.normal(streams_of[3], (D,), jnp.float32), 0.5, 1.5).astype(jnp.bfloat16)
    qkv_weight_one = bell_draw(streams_of[4], (3, D, D), D ** -0.5, 0.21875, ((1, 8), (2, 4)))
    out_weight_one = bell_draw(streams_of[5], (D, D), (D // 8) ** -0.5, 0.625, ((0, 4), (1, 8)))
    first_feedforward_gain = jnp.clip(1.0 + 0.1 * jax.random.normal(streams_of[6], (D,), jnp.float32), 0.5, 1.5).astype(jnp.bfloat16)
    up_weight_one = bell_draw(streams_of[7], (D, FF), D ** -0.5, 0.21875, ((0, 8), (1, 4)))
    down_weight_one = bell_draw(streams_of[8], (FF, D), (FF // 2) ** -0.5, 0.15625, ((0, 4), (1, 8)))
    attn_gain_two = jnp.clip(1.0 + 0.1 * jax.random.normal(streams_of[9], (D,), jnp.float32), 0.5, 1.5).astype(jnp.bfloat16)
    qkv_weight_two = bell_draw(streams_of[10], (3, D, D), D ** -0.5, 0.21875, ((1, 8), (2, 4)))
    out_weight_two = bell_draw(streams_of[11], (D, D), (D // 8) ** -0.5, 0.625, ((0, 4), (1, 8)))
    moe_gain_two = jnp.clip(1.0 + 0.1 * jax.random.normal(streams_of[12], (D,), jnp.float32), 0.5, 1.5).astype(jnp.bfloat16)
    router_weight = bell_draw(streams_of[13], (D, E), (2 * D) ** -0.5, 0.15625, ((0, 8),))
    expert_up = bell_draw(streams_of[14], (E, D, FF), D ** -0.5, 0.21875, ((1, 8), (2, 4)))
    expert_down = bell_draw(streams_of[15], (E, FF, D), (FF // 8) ** -0.5, 0.3125, ((1, 4), (2, 8)))
    cotangent = bell_draw(streams_of[16], (IMAGES, SEQ, D), 1.0, 6.0, ((0, 8),), jnp.float32)
    return dict(activations=activations, image_live=image_live, expert_routes=expert_routes, attn_gain_one=attn_gain_one, qkv_weight_one=qkv_weight_one, out_weight_one=out_weight_one, first_feedforward_gain=first_feedforward_gain, up_weight_one=up_weight_one, down_weight_one=down_weight_one, attn_gain_two=attn_gain_two, qkv_weight_two=qkv_weight_two, out_weight_two=out_weight_two, moe_gain_two=moe_gain_two, router_weight=router_weight, expert_up=expert_up, expert_down=expert_down, cotangent=cotangent)


@jax.custom_vjp
def low(v):
    return lax.optimization_barrier(v.astype(jnp.bfloat16)).astype(jnp.float32)

@jax.custom_vjp
def low_back(v):
    return v

def low_keep(v):
    return (low(v), None)

def low_pass(kept, grad):
    return (grad,)

def back_keep(v):
    return (v, None)

def back_low(kept, grad):
    return (low(grad),)
low.defvjp(low_keep, low_pass)
low_back.defvjp(back_keep, back_low)
highest = lax.Precision.HIGHEST
epsilon = 1e-06

def norm_gain(field, gain_vec):
    centred = field - lax.optimization_barrier(jnp.mean(field, axis=-1, keepdims=True))
    spread = lax.optimization_barrier(jnp.mean(centred * centred, axis=-1, keepdims=True))
    return centred * lax.rsqrt(spread + epsilon) * gain_vec

def gelu(field):
    return 0.5 * field * (1.0 + jax.scipy.special.erf(field * 0.7071067811865476))

def attend(field, gain_vec, weight_qkv, weight_out):
    batch_size, length, model_width = field.shape
    normed = low(norm_gain(field, gain_vec))
    packed = low_back(low(jnp.einsum('bsd,tde->tbse', normed, weight_qkv, precision=highest)))
    packed = packed.reshape(3, batch_size, length, NH, HD)
    scores = low_back(jnp.einsum('bqhe,bkhe->bhqk', packed[0], packed[1], precision=highest) * HD ** (-0.5))
    prob_table = low(jax.nn.softmax(scores, axis=-1))
    mixed_heads = low_back(low(jnp.einsum('bhqk,bkhe->bqhe', prob_table, packed[2], precision=highest)))
    mixed_heads = mixed_heads.reshape(batch_size, length, model_width)
    return field + low_back(jnp.einsum('bse,ed->bsd', mixed_heads, weight_out, precision=highest))

def feed(field, gain_vec, weight_up, weight_down):
    normed = low(norm_gain(field, gain_vec))
    hidden = low_back(jnp.matmul(normed, weight_up, precision=highest))
    active = low(gelu(hidden))
    return field + low_back(jnp.matmul(active, weight_down, precision=highest))

def experts_layer(field, gain_vec, weight_router, weight_up, weight_down, route_ids):
    normed = low(norm_gain(field, gain_vec))
    prob_table = jax.nn.softmax(jnp.matmul(normed, weight_router, precision=highest), axis=-1)
    gate_values = jnp.take_along_axis(prob_table, route_ids, axis=-1)
    picks = (route_ids[..., None] == jnp.arange(E, dtype=jnp.int32)).astype(prob_table.dtype)
    combine = lax.optimization_barrier(jnp.sum(gate_values[..., None] * picks, axis=-2))
    output = field
    for expert in range(E):
        hidden = low_back(jnp.matmul(normed, weight_up[expert], precision=highest))
        active = low(gelu(hidden))
        expert_out = low_back(jnp.matmul(active, weight_down[expert], precision=highest))
        output = output + combine[..., expert:expert + 1] * expert_out
    return output

def block(weights, field, route_ids):
    gain_a, qkv_a, out_a, gain_b, up_b, down_b, gain_c, qkv_c, out_c, gain_d, router_d, up_d, down_d = weights
    field = attend(field, gain_a, qkv_a, out_a)
    field = feed(field, gain_b, up_b, down_b)
    field = attend(field, gain_c, qkv_c, out_c)
    return experts_layer(field, gain_d, router_d, up_d, down_d, route_ids)

def reference(activations, image_live, expert_routes, attn_gain_one, qkv_weight_one, out_weight_one, first_feedforward_gain, up_weight_one, down_weight_one, attn_gain_two, qkv_weight_two, out_weight_two, moe_gain_two, router_weight, expert_up, expert_down, cotangent):
    weights = tuple((item.astype(jnp.float32) for item in (attn_gain_one, qkv_weight_one, out_weight_one, first_feedforward_gain, up_weight_one, down_weight_one, attn_gain_two, qkv_weight_two, out_weight_two, moe_gain_two, router_weight, expert_up, expert_down)))
    groups = activations.shape[0] // IMG_DEV
    blocks_in = activations.reshape(groups, IMG_DEV, SEQ, D)
    blocks_route = expert_routes.reshape(groups, IMG_DEV, SEQ, 2).astype(jnp.int32)
    stepper = jax.checkpoint(block)

    def forward(weight_set, inputs):

        def one_group(pair):
            return stepper(weight_set, pair[0], pair[1])
        return lax.map(one_group, (inputs, blocks_route))
    output, pull = jax.vjp(forward, weights, blocks_in)
    keep_mask = image_live.astype(cotangent.dtype)[:, None, None]
    grads, input_blocks = pull((cotangent * keep_mask).reshape(blocks_in.shape))
    return (output.reshape(activations.shape), input_blocks.reshape(activations.shape), grads[0], grads[1], grads[2], grads[3], grads[4], grads[5], grads[6], grads[7], grads[8], grads[9], grads[10], grads[11], grads[12])
```

```python
import functools

import jax
import jax.numpy as jnp
from jax import lax
from jax.experimental import pallas as pl
from jax.experimental.pallas import tpu as pltpu
from jax.sharding import PartitionSpec as P

HD = 64
PLANES = 4
epsilon = 1e-06
root_half = 0.7071067811865476
inv_root_two_pi = 0.3989422804014327
highest = lax.Precision.HIGHEST
bf16 = jnp.bfloat16
f32 = jnp.float32


def nn(a, b):
    return lax.dot_general(a, b, (((1,), (0,)), ((), ())), preferred_element_type=f32)


def nt(a, b):
    return lax.dot_general(a, b, (((1,), (1,)), ((), ())), preferred_element_type=f32)


def tn(a, b):
    return lax.dot_general(a, b, (((0,), (0,)), ((), ())), preferred_element_type=f32)


def norm_parts(x):
    c = x - jnp.mean(x, axis=-1, keepdims=True)
    rs = lax.rsqrt(jnp.mean(c * c, axis=-1, keepdims=True) + epsilon)
    return c * rs, rs


def norm_pull(x, gain, dh):
    hat, rs = norm_parts(x)
    t = dh * gain
    mean_t = jnp.mean(t, axis=-1, keepdims=True)
    mean_th = jnp.mean(t * hat, axis=-1, keepdims=True)
    return rs * (t - mean_t - hat * mean_th), jnp.sum(dh * hat, axis=0, keepdims=True)


def join_halves(core, own, other):
    low = jnp.where(core == 0, own, other)
    high = jnp.where(core == 0, other, own)
    return jnp.concatenate([low, high], axis=1)


def split_halves(core, full):
    half = full.shape[1] // 2
    low, high = full[:, :half], full[:, half:]
    return jnp.where(core == 0, low, high), jnp.where(core == 0, high, low)


def row_of(index, shape):
    return lax.broadcasted_iota(jnp.int32, shape, 0) == index


def assemble(dst, me, refs, pick=()):
    parts = len(refs)
    rows = dst.shape[0] // (parts * PLANES)
    for a, ref in enumerate(refs):
        for m in range(PLANES):
            start = pl.multiple_of((me ^ (m * parts + a)) * rows, rows)
            dst[pl.ds(start, rows), :] = ref[(m,) + pick].astype(dst.dtype)


def scatter_blocks(src, me, refs, pick=()):
    parts = len(refs)
    rows = src.shape[0] // (parts * PLANES)
    for a, ref in enumerate(refs):
        for m in range(PLANES):
            start = pl.multiple_of((me ^ (m * parts + a)) * rows, rows)
            ref[(m,) + pick] = src[pl.ds(start, rows), :].astype(ref.dtype)


def head_tiles(y, head):
    at = 256 * head
    qk, vt = y[:, at : at + 128], y[:, at + 128 : at + 256]
    low = lax.broadcasted_iota(jnp.int32, qk.shape, 1) < HD
    q = jnp.where(low, qk, 0.0).astype(bf16)
    k = jnp.where(low, pltpu.roll(qk, HD, 1), 0.0).astype(bf16)
    v = jnp.where(low, 0.0, pltpu.roll(vt, HD, 1)).astype(bf16)
    return q, k, v


def probs_of(q, k, tokens):
    s = nt(q, k) * (HD**-0.5)
    s = jnp.where(lax.broadcasted_iota(jnp.int32, s.shape, 1) < tokens, s, -1e30)
    e = jnp.exp(s - jnp.max(s, axis=-1, keepdims=True))
    return e / jnp.sum(e, axis=-1, keepdims=True)


def attn_fwd_kernel(tokens, parts, gain_row, first, scal, *refs):
    me, core = scal[0], scal[1]
    refs = list(refs)
    x_ref = refs.pop(0)
    if first:
        x = x_ref[...]
    else:
        own, other, rows_ref = refs.pop(0), refs.pop(0), refs.pop(0)
        x = x_ref[...] + join_halves(core, own[...], other[...])
    blocks = [refs.pop(0) for _ in range(parts)]
    if first:
        keep_ref, send_ref, rows_ref, w = refs
    else:
        x_out, keep_ref, send_ref, w = refs
    assemble(w, me, blocks)
    model = w.shape[0]
    if first:
        eye = (
            lax.broadcasted_iota(jnp.int32, (8, 128), 0)
            == lax.broadcasted_iota(jnp.int32, (8, 128), 1)
        ).astype(bf16)
        rows_ref[...] = nt(eye, w[:, model:].astype(bf16))
    else:
        x_out[...] = x
    hat, _ = norm_parts(x)
    h = (hat * rows_ref[gain_row : gain_row + 1, :]).astype(bf16)
    y = nn(h, w[:, :model].astype(bf16))
    branch = jnp.zeros(x.shape, f32)
    for head in range(model // 256):
        q, k, v = head_tiles(y, head)
        p = probs_of(q, k, tokens).astype(bf16)
        o = nn(p, v).astype(bf16)
        at = 256 * head + 128
        branch += nt(o, w[:, at : at + 128].astype(bf16))
    keep, send = split_halves(core, branch)
    keep_ref[...] = keep
    send_ref[...] = send.astype(send_ref.dtype)


def mlp_fwd_kernel(parts, gain_row, scal, x_ref, own, other, rows_ref, *refs):
    me, core = scal[0], scal[1]
    blocks, (x_out, keep_ref, send_ref, up, down) = refs[:parts], refs[parts:]
    assemble(up, me, blocks, (0,))
    assemble(down, me, blocks, (1,))
    x = x_ref[...] + join_halves(core, own[...], other[...])
    x_out[...] = x
    hat, _ = norm_parts(x)
    h = (hat * rows_ref[gain_row : gain_row + 1, :]).astype(bf16)
    u = nn(h, up[...].astype(bf16))
    r = (0.5 * u * (1.0 + lax.erf(u * root_half))).astype(bf16)
    keep, send = split_halves(core, nt(r, down[...].astype(bf16)))
    keep_ref[...] = keep
    send_ref[...] = send.astype(send_ref.dtype)


def router_probs(h, rows_ref):
    logits = nt(h, rows_ref[...].astype(bf16))
    lane = lax.broadcasted_iota(jnp.int32, logits.shape, 1)
    logits = jnp.where(lane < PLANES, logits, -1e30)
    e = jnp.exp(logits - jnp.max(logits, axis=-1, keepdims=True))
    return e / jnp.sum(e, axis=-1, keepdims=True), lane


def routed(routes, lane):
    return (routes[:, 0:1] == lane) | (routes[:, 1:2] == lane)


def moe_pre_kernel(tokens, gain_row, scal, x_ref, own, other, rows_ref, routes, x_out, h_out, half_out):
    core = scal[1]
    x = x_ref[...] + join_halves(core, own[...], other[...])
    x_out[...] = x
    hat, _ = norm_parts(x)
    h = (hat * rows_ref[gain_row : gain_row + 1, :]).astype(bf16)
    probs, lane = router_probs(h, rows_ref)
    gates = jnp.where(routed(routes[...], lane), probs, 0.0).astype(bf16)
    eye = (
        lax.broadcasted_iota(jnp.int32, (8, 8), 0) == lax.broadcasted_iota(jnp.int32, (8, 8), 1)
    ).astype(bf16)
    gate_rows = nt(eye, gates)
    padded, model = x.shape
    half = model // 2
    live = lax.broadcasted_iota(jnp.int32, x.shape, 0) < tokens
    h = jnp.where(live, h.astype(f32), 0.0)
    wide = jnp.concatenate([gate_rows, jnp.zeros((8, half - padded), f32)], axis=1)
    block = jnp.concatenate([jnp.zeros((padded - 8, half), f32), wide], axis=0)
    low, high = h[:, :half] + block, h[:, half:] + block
    h_out[...] = jnp.concatenate([low, high], axis=1).astype(bf16)
    half_out[...] = jnp.where(core == 0, low, high).astype(bf16)


def moe_kernel(parts, scal, *refs):
    me, core, expert = scal[0], scal[1], scal[2]
    refs = list(refs)
    h_refs = [refs.pop(0) for _ in range(1 + 2 * (PLANES - 1))]
    g_refs = [refs.pop(0) for _ in range(1 + 2 * (PLANES - 1))]
    blocks = [refs.pop(0) for _ in range(parts)]
    y_keep, y_send, d_keep, d_send = [refs.pop(0) for _ in range(4)]
    grads = [refs.pop(0) for _ in range(parts)]
    up, down, hs, gs, rs, dus, dys, acc = refs
    assemble(up, me, blocks, (0,))
    assemble(down, me, blocks, (1,))
    for dst, src in ((hs, h_refs), (gs, g_refs)):
        dst[0] = src[0][...]
        for m in range(1, PLANES):
            dst[m] = join_halves(core, src[m][...], src[PLANES - 1 + m][...])
    padded, model = hs.shape[1:]
    half = model // 2

    def step(m, carry):
        h, g = hs[m], gs[m]
        rows = h.astype(f32)[padded - 8 :, :256]
        pick = row_of(expert, (8, 128)).astype(f32)
        gate = tn(rows, pick)[:padded, :1]
        u = nn(h, up[...].astype(bf16))
        cdf = 0.5 * (1.0 + lax.erf(u * root_half))
        r = (u * cdf).astype(bf16)
        t = nn(g, down[...].astype(bf16))
        slope = cdf + u * inv_root_two_pi * jnp.exp(-0.5 * u * u)
        du = (gate * t * slope).astype(bf16)
        rs[m] = r
        dus[m] = du
        dys[m] = (gate * g.astype(f32)).astype(bf16)
        dots = nt(jnp.ones((8, r.shape[1]), bf16), (r.astype(f32) * t).astype(bf16))
        dots = jnp.where(row_of(expert, dots.shape), dots, 0.0)
        y = gate * nt(r, down[...].astype(bf16))
        keep, send = split_halves(core, y)
        y_keep[m] = keep
        y_send[m] = send.astype(y_send.dtype)
        dh = nt(du, up[...].astype(bf16))
        wide = jnp.concatenate([dots, jnp.zeros((8, model - padded), f32)], axis=1)
        dh = dh + jnp.concatenate([jnp.zeros((padded - 8, model), f32), wide], axis=0)
        keep, send = split_halves(core, dh)
        d_keep[m] = keep
        d_send[m] = send.astype(d_send.dtype)
        return carry

    lax.fori_loop(0, PLANES, step, 0)
    flat = (PLANES * padded, model)
    acc[...] = tn(hs[...].reshape(flat), dus[...].reshape(flat))
    scatter_blocks(acc, me, grads, (0,))
    acc[...] = tn(dys[...].reshape(flat), rs[...].reshape(flat))
    scatter_blocks(acc, me, grads, (1,))


def plain_pull(x_ref, own, other, g_ref, rows_ref, small_ref, gain_row, core):
    dh = join_halves(core, own[...], other[...])
    dx, dgain = norm_pull(x_ref[...], rows_ref[gain_row : gain_row + 1, :], dh)
    small = small_ref[...] + jnp.where(row_of(gain_row, small_ref.shape), dgain, 0.0)
    return g_ref[...] + dx, small


def router_pull(tokens, x_ref, own, other, g_ref, rows_ref, routes, gain_row, core):
    dh = join_halves(core, own[...], other[...])
    padded, model = dh.shape
    gain = rows_ref[gain_row : gain_row + 1, :]
    hat, _ = norm_parts(x_ref[...])
    live = lax.broadcasted_iota(jnp.int32, dh.shape, 0) < tokens
    h = (hat * gain).astype(bf16)
    probs, lane = router_probs(h, rows_ref)
    dots = dh[padded - 8 :, :256]
    eye = (
        lax.broadcasted_iota(jnp.int32, (8, 8), 0) == lax.broadcasted_iota(jnp.int32, (8, 8), 1)
    ).astype(f32)
    dprobs = lax.dot_general(
        dots, eye, (((0,), (0,)), ((), ())), precision=highest, preferred_element_type=f32
    )[:padded]
    keep = routed(routes[...], lane) & (lax.broadcasted_iota(jnp.int32, lane.shape, 0) < tokens)
    dprobs = jnp.where(keep, dprobs, 0.0)
    dlogits = probs * (dprobs - jnp.sum(probs * dprobs, axis=-1, keepdims=True))
    small = lax.dot_general(
        dlogits, h.astype(f32), (((0,), (0,)), ((), ())), precision=highest, preferred_element_type=f32
    )
    router = jnp.where(lax.broadcasted_iota(jnp.int32, small.shape, 0) < PLANES, rows_ref[...], 0.0)
    dh = jnp.where(live, dh, 0.0) + lax.dot_general(
        dlogits, router, (((1,), (0,)), ((), ())), precision=highest, preferred_element_type=f32
    )
    dx, dgain = norm_pull(x_ref[...], gain, dh)
    small = small + jnp.where(row_of(gain_row, small.shape), dgain, 0.0)
    return g_ref[...] + dx, small


def attn_bwd_kernel(tokens, parts, rows_at, last, scal, *refs):
    me, core = scal[0], scal[1]
    refs = list(refs)
    x_up, own, other, g_ref, rows_ref, extra, x_ref = [refs.pop(0) for _ in range(7)]
    blocks = [refs.pop(0) for _ in range(parts)]
    g_out, small_out, keep_ref, send_ref = [refs.pop(0) for _ in range(4)]
    grads = [refs.pop(0) for _ in range(parts)]
    w, acc = refs
    assemble(w, me, blocks)
    up_row, gain_row = rows_at
    if last:
        g, small = plain_pull(x_up, own, other, g_ref, rows_ref, extra, up_row, core)
    else:
        g, small = router_pull(tokens, x_up, own, other, g_ref, rows_ref, extra, up_row, core)
    g_out[...] = g
    small_out[...] = small
    model = acc.shape[1]
    hat, _ = norm_parts(x_ref[...])
    h = (hat * rows_ref[gain_row : gain_row + 1, :]).astype(bf16)
    db = g.astype(bf16)
    y = nn(h, w[:, :model].astype(bf16))
    dh = jnp.zeros(g.shape, f32)
    left, right = [], []
    for head in range(model // 256):
        at = 256 * head
        q, k, v = head_tiles(y, head)
        p = probs_of(q, k, tokens)
        pb = p.astype(bf16)
        o = nn(pb, v).astype(bf16)
        wqk = w[:, at : at + 128].astype(bf16)
        wvo = w[:, at + 128 : at + 256].astype(bf16)
        do = nn(db, wvo)
        low = lax.broadcasted_iota(jnp.int32, do.shape, 1) < HD
        do = jnp.where(low, 0.0, do).astype(bf16)
        dp = nt(do, v)
        dv = tn(pb, do)
        ds = (p * (dp - jnp.sum(p * dp, axis=-1, keepdims=True))).astype(bf16)
        dq = nn(ds, k) * (HD**-0.5)
        dk = tn(ds, q) * (HD**-0.5)
        dqk = (dq + pltpu.roll(dk, HD, 1)).astype(bf16)
        dvt = pltpu.roll(dv, HD, 1).astype(bf16)
        dh += nt(dqk, wqk) + nt(dvt, wvo)
        left += [dqk, dvt]
        right += [jnp.zeros_like(o), o]
    keep, send = split_halves(core, dh)
    keep_ref[...] = keep
    send_ref[...] = send.astype(send_ref.dtype)
    acc[...] = tn(h, jnp.concatenate(left, axis=1)) + tn(db, jnp.concatenate(right, axis=1))
    scatter_blocks(acc, me, grads)


def mlp_bwd_kernel(parts, rows_at, scal, x_up, own, other, g_ref, rows_ref, extra, x_ref, *refs):
    me, core = scal[0], scal[1]
    refs = list(refs)
    blocks = [refs.pop(0) for _ in range(parts)]
    g_out, small_out, keep_ref, send_ref = [refs.pop(0) for _ in range(4)]
    grads = [refs.pop(0) for _ in range(parts)]
    up, down, acc = refs
    assemble(up, me, blocks, (0,))
    assemble(down, me, blocks, (1,))
    up_row, gain_row = rows_at
    g, small = plain_pull(x_up, own, other, g_ref, rows_ref, extra, up_row, core)
    g_out[...] = g
    small_out[...] = small
    hat, _ = norm_parts(x_ref[...])
    h = (hat * rows_ref[gain_row : gain_row + 1, :]).astype(bf16)
    dm = g.astype(bf16)
    u = nn(h, up[...].astype(bf16))
    cdf = 0.5 * (1.0 + lax.erf(u * root_half))
    r = (u * cdf).astype(bf16)
    slope = cdf + u * inv_root_two_pi * jnp.exp(-0.5 * u * u)
    du = (nn(dm, down[...].astype(bf16)) * slope).astype(bf16)
    keep, send = split_halves(core, nt(du, up[...].astype(bf16)))
    keep_ref[...] = keep
    send_ref[...] = send.astype(send_ref.dtype)
    acc[...] = tn(h, du)
    scatter_blocks(acc, me, grads, (0,))
    acc[...] = tn(dm, r)
    scatter_blocks(acc, me, grads, (1,))


def final_kernel(tokens, gain_row, scal, x_ref, own, other, g_ref, rows_ref, extra, g_out, *refs):
    me, core = scal[0], scal[1]
    grads, acc = refs[:-1], refs[-1]
    g, small = plain_pull(x_ref, own, other, g_ref, rows_ref, extra, gain_row, core)
    g_out[...] = g[:tokens]
    eye = (
        lax.broadcasted_iota(jnp.int32, (8, 128), 0) == lax.broadcasted_iota(jnp.int32, (8, 128), 1)
    ).astype(f32)
    acc[...] = lax.dot_general(
        small, eye, (((0,), (0,)), ((), ())), precision=highest, preferred_element_type=f32
    )
    scatter_blocks(acc, me, grads)


def run(kernel, scal, ins, outs, scratch, flops):
    vmem = pl.BlockSpec(memory_space=pltpu.VMEM)
    size = lambda s: s.size * s.dtype.itemsize
    return pl.pallas_call(
        kernel,
        out_shape=outs,
        in_specs=[pl.BlockSpec(memory_space=pltpu.SMEM)] + [vmem] * len(ins),
        out_specs=[vmem] * len(outs),
        scratch_shapes=scratch,
        compiler_params=pltpu.CompilerParams(vmem_limit_bytes=48 * 2**20),
        cost_estimate=pl.CostEstimate(
            flops=int(flops),
            bytes_accessed=int(sum(size(a) for a in ins) + sum(size(o) for o in outs)),
            transcendentals=0,
        ),
    )(scal, *ins)


def shape(dims, kind):
    return jax.ShapeDtypeStruct(tuple(dims), kind)


def tie(value, *after):
    return lax.optimization_barrier((value,) + after)[0]


def shards(
    fsdp,
    tensor,
    activations,
    image_live,
    expert_routes,
    attn_gain_one,
    qkv_weight_one,
    out_weight_one,
    first_feedforward_gain,
    up_weight_one,
    down_weight_one,
    attn_gain_two,
    qkv_weight_two,
    out_weight_two,
    moe_gain_two,
    router_weight,
    expert_up,
    expert_down,
    cotangent,
):
    parts = fsdp // PLANES
    tokens, model = activations.shape[1:]
    padded = -(-(tokens + 8) // 16) * 16
    half = model // 2
    rows = model // fsdp
    heads = qkv_weight_one.shape[2] // HD
    hidden = up_weight_one.shape[1]
    held = bf16 if rows % 16 == 0 else f32
    me = lax.axis_index("fsdp")
    place = lax.axis_index("tensor")
    core, plane = place % 2, me // parts
    scal = jnp.stack([me, core, plane, place]).astype(jnp.int32)

    def across(value, k):
        return lax.ppermute(value, "fsdp", [(i, i ^ k) for i in range(fsdp)])

    def over(value, k):
        return lax.ppermute(value, "tensor", [(i, i ^ k) for i in range(tensor)])

    def spread(stacked):
        arrays, bit = [stacked], 1
        while bit < parts:
            arrays += [across(a, bit) for a in arrays]
            bit *= 2
        return arrays

    def gather_planes(block):
        return jnp.stack([block] + [across(block, m * parts) for m in range(1, PLANES)])

    def fold(arrays):
        arrays, bit = list(arrays), parts // 2
        while bit:
            for a in range(bit):
                arrays[a] = arrays[a].astype(f32) + across(arrays[a + bit].astype(bf16), bit).astype(f32)
            bit //= 2
        return arrays[0]

    def reduce_planes(stacked):
        total = stacked[0].astype(f32)
        for m in range(1, PLANES):
            total = total + across(stacked[m].astype(bf16), m * parts).astype(f32)
        return total

    def pair(total):
        low = total.astype(bf16)
        total = low.astype(f32) + over(low, 2).astype(f32)
        return total, over(total, 1)

    def joined(keep, send):
        return pair(keep + over(send, 1))

    def attn_pack(qkv, out):
        by_head = jnp.moveaxis(qkv.reshape(3, rows, heads, HD), 0, 2)
        out = out.reshape(heads, HD, rows).transpose(2, 0, 1)[:, :, None]
        return jnp.concatenate([by_head, out], axis=2).reshape(rows, heads * 4 * HD)

    def attn_unpack(grad):
        grad = grad.reshape(rows, heads, 4, HD)
        qkv = jnp.moveaxis(grad[:, :, :3], 2, 0).reshape(3, rows, heads * HD)
        return qkv, grad[:, :, 3].transpose(1, 2, 0).reshape(heads * HD, rows)

    smalls = jnp.concatenate(
        [
            router_weight,
            attn_gain_one[:, None],
            first_feedforward_gain[:, None],
            attn_gain_two[:, None],
            moe_gain_two[:, None],
        ],
        axis=1,
    )
    smalls = jnp.pad(smalls, ((0, 0), (0, 128 - smalls.shape[1])))
    one = jnp.concatenate([attn_pack(qkv_weight_one, out_weight_one), smalls], axis=1)
    one = gather_planes(one)
    w_one = spread(one)
    mlp = jnp.stack([up_weight_one, down_weight_one.T])
    mlp = gather_planes(tie(mlp, one))
    w_mlp = spread(mlp)
    two = gather_planes(tie(attn_pack(qkv_weight_two, out_weight_two), mlp))
    w_two = spread(two)
    experts = jnp.stack([expert_up, jnp.swapaxes(expert_down, 1, 2)], axis=1)
    experts = tie(experts, two)
    mine = [lax.dynamic_index_in_dim(experts, plane ^ m, 0, keepdims=False) for m in range(PLANES)]
    mine = jnp.stack([mine[0]] + [across(mine[m], m * parts) for m in range(1, PLANES)])
    w_moe = spread(mine)

    def image_blocks(own, own_half):
        near = [across(own_half, m * parts) for m in range(1, PLANES)]
        return [own] + near + [over(n, 1) for n in near]

    pad = ((0, padded - tokens), (0, 0))
    stream0 = jnp.pad(activations[0], pad)
    grad3 = jnp.pad(cotangent[0] * image_live[0].astype(f32), pad)
    routes = jnp.pad(expert_routes[0], pad, constant_values=-1)
    grad_low = tie(grad3.astype(bf16), mine)
    grad_half = jnp.where(core == 0, grad_low[:, :half], grad_low[:, half:])
    g_blocks = image_blocks(grad_low, grad_half)

    stream = shape((padded, model), f32)
    pieces = [shape((padded, half), f32)] * 2
    wide = pltpu.VMEM((model, model + 128), held)
    square = pltpu.VMEM((model, model), held)
    total = pltpu.VMEM((model, model), f32)
    unit = 2 * padded * model * model

    keep, send, small_rows = run(
        functools.partial(attn_fwd_kernel, tokens, parts, 4, True),
        scal,
        [stream0] + w_one,
        pieces + [shape((8, model), f32)],
        [wide],
        3 * unit,
    )
    own, other = joined(keep, send)
    stream1, keep, send = run(
        functools.partial(mlp_fwd_kernel, parts, 5),
        scal,
        [stream0, own, other, small_rows] + w_mlp,
        [stream] + pieces,
        [square, square],
        2 * unit,
    )
    own, other = joined(keep, send)
    stream2, keep, send = run(
        functools.partial(attn_fwd_kernel, tokens, parts, 6, False),
        scal,
        [stream1, own, other, small_rows] + w_two,
        [stream] + pieces,
        [square],
        3 * unit,
    )
    own, other = joined(keep, send)
    stream3, h_full, h_half = run(
        functools.partial(moe_pre_kernel, tokens, 7),
        scal,
        [stream2, own, other, small_rows, routes],
        [stream, shape((padded, model), bf16), shape((padded, half), bf16)],
        [],
        unit / 50,
    )
    h_blocks = image_blocks(h_full, h_half)
    images = pltpu.VMEM((PLANES, padded, model), bf16)
    image_hidden = pltpu.VMEM((PLANES, padded, hidden), bf16)
    block_pieces = [shape((PLANES, padded, half), f32), shape((PLANES, padded, half), bf16)]
    y_keep, y_send, d_keep, d_send, *expert_grads = run(
        functools.partial(moe_kernel, parts),
        scal,
        h_blocks + g_blocks + w_moe,
        block_pieces * 2 + [shape((PLANES, 2, rows, hidden), bf16)] * parts,
        [square, square, images, images, image_hidden, image_hidden, images, total],
        24 * unit,
    )

    def home(keep, send):
        summed = keep + over(send, 1).astype(f32)
        return pair(reduce_planes(summed))

    own, other = home(d_keep, d_send)
    block_grads = [shape((PLANES, rows, model), bf16)] * parts
    grad2, small, keep, send, *two_grads = run(
        functools.partial(attn_bwd_kernel, tokens, parts, (7, 6), False),
        scal,
        [stream3, own, other, grad3, small_rows, routes, stream2] + w_two,
        [stream, shape((8, model), f32)] + pieces + block_grads,
        [square, total],
        8 * unit,
    )
    own, other = joined(keep, send)
    y_keep, y_send = lax.optimization_barrier((y_keep, y_send, keep))[:2]
    y_own, y_other = home(y_keep, y_send)
    expert_sum = fold(expert_grads)
    grad1, small, keep, send, *mlp_grads = run(
        functools.partial(mlp_bwd_kernel, parts, (6, 5)),
        scal,
        [stream2, own, other, grad2, small_rows, small, stream1] + w_mlp,
        [stream, shape((8, model), f32)]
        + pieces
        + [shape((PLANES, 2, rows, hidden), bf16)] * parts,
        [square, square, total],
        5 * unit,
    )
    own, other = joined(keep, send)
    grad0, small, keep, send, *one_grads = run(
        functools.partial(attn_bwd_kernel, tokens, parts, (5, 4), True),
        scal,
        [stream1, own, other, grad1, small_rows, small, stream0] + w_one,
        [stream, shape((8, model), f32)] + pieces + block_grads,
        [wide, total],
        8 * unit,
    )
    own, other = joined(keep, send)
    input_grad, *small_grads = run(
        functools.partial(final_kernel, tokens, 4),
        scal,
        [stream0, own, other, grad0, small_rows, small],
        [shape((tokens, model), f32)] + [shape((PLANES, rows, 128), bf16)] * parts,
        [pltpu.VMEM((model, 128), f32)],
        unit / 50,
    )

    low = jnp.where(core == 0, y_own, y_other)
    high = jnp.where(core == 0, y_other, y_own)
    result = (stream3 + jnp.concatenate([low, high], axis=1))[:tokens]

    came = [expert_sum[0]]
    for m in range(1, PLANES):
        came.append(across(expert_sum[m].astype(bf16), m * parts).astype(f32))
    bit0, bit1 = plane % 2 == 1, plane // 2 == 1

    def of_expert(x):
        a, b = jnp.where(bit0, came[x ^ 1], came[x]), jnp.where(bit0, came[x ^ 3], came[x ^ 2])
        return jnp.where(bit1, b, a)

    by_expert = jnp.stack([of_expert(x) for x in range(PLANES)])
    two_sum = reduce_planes(fold(two_grads))
    mlp_sum = reduce_planes(fold(mlp_grads))
    one_sum = reduce_planes(fold(one_grads))
    small_sum = reduce_planes(fold(small_grads))
    qkv_one, out_one = attn_unpack(one_sum)
    qkv_two, out_two = attn_unpack(two_sum)
    return (
        result[None],
        input_grad[None],
        small_sum[:, 4],
        qkv_one,
        out_one,
        small_sum[:, 5],
        mlp_sum[0],
        mlp_sum[1].T,
        small_sum[:, 6],
        qkv_two,
        out_two,
        small_sum[:, 7],
        small_sum[:, :PLANES],
        by_expert[:, 0],
        jnp.swapaxes(by_expert[:, 1], 1, 2),
    )


def solution(mesh):
    return jax.shard_map(
        functools.partial(shards, mesh.shape["fsdp"], mesh.shape["tensor"]),
        mesh=mesh,
        in_specs=(
            P("fsdp", None, None),
            P("fsdp"),
            P("fsdp", None, None),
            P("fsdp"),
            P(None, "fsdp", "tensor"),
            P("tensor", "fsdp"),
            P("fsdp"),
            P("fsdp", "tensor"),
            P("tensor", "fsdp"),
            P("fsdp"),
            P(None, "fsdp", "tensor"),
            P("tensor", "fsdp"),
            P("fsdp"),
            P("fsdp", None),
            P(None, "fsdp", "tensor"),
            P(None, "tensor", "fsdp"),
            P("fsdp", None, None),
        ),
        out_specs=(
            P("fsdp", None, None),
            P("fsdp", None, None),
            P("fsdp"),
            P(None, "fsdp", "tensor"),
            P("tensor", "fsdp"),
            P("fsdp"),
            P("fsdp", "tensor"),
            P("tensor", "fsdp"),
            P("fsdp"),
            P(None, "fsdp", "tensor"),
            P("tensor", "fsdp"),
            P("fsdp"),
            P("fsdp", None),
            P(None, "fsdp", "tensor"),
            P(None, "tensor", "fsdp"),
        ),
        check_vma=False,
    )
```

```python
import functools

import jax
import jax.numpy as jnp
from jax import lax
from jax.experimental import pallas as pl
from jax.experimental.pallas import tpu as pltpu
from jax.sharding import PartitionSpec as P

HD = 64
PLANES = 4
epsilon = 1e-06
root_half = 0.7071067811865476
inv_root_two_pi = 0.3989422804014327
highest = lax.Precision.HIGHEST
bf16 = jnp.bfloat16
f32 = jnp.float32


def nn(a, b):
    return lax.dot_general(a, b, (((1,), (0,)), ((), ())), preferred_element_type=f32)


def nt(a, b):
    return lax.dot_general(a, b, (((1,), (1,)), ((), ())), preferred_element_type=f32)


def tn(a, b):
    return lax.dot_general(a, b, (((0,), (0,)), ((), ())), preferred_element_type=f32)


def norm_parts(x):
    c = x - jnp.mean(x, axis=-1, keepdims=True)
    rs = lax.rsqrt(jnp.mean(c * c, axis=-1, keepdims=True) + epsilon)
    return c * rs, rs


def norm_pull(x, gain, dh):
    hat, rs = norm_parts(x)
    t = dh * gain
    mean_t = jnp.mean(t, axis=-1, keepdims=True)
    mean_th = jnp.mean(t * hat, axis=-1, keepdims=True)
    return rs * (t - mean_t - hat * mean_th), jnp.sum(dh * hat, axis=0, keepdims=True)


def join_halves(core, own, other):
    low = jnp.where(core == 0, own, other)
    high = jnp.where(core == 0, other, own)
    return jnp.concatenate([low, high], axis=1)


def split_halves(core, full):
    half = full.shape[1] // 2
    low, high = full[:, :half], full[:, half:]
    return jnp.where(core == 0, low, high), jnp.where(core == 0, high, low)


def row_of(index, shape):
    return lax.broadcasted_iota(jnp.int32, shape, 0) == index


def assemble(dst, me, refs, pick=()):
    parts = len(refs)
    rows = dst.shape[0] // (parts * PLANES)
    for a, ref in enumerate(refs):
        for m in range(PLANES):
            start = pl.multiple_of((me ^ (m * parts + a)) * rows, rows)
            dst[pl.ds(start, rows), :] = ref[(m,) + pick].astype(dst.dtype)


def scatter_blocks(src, me, refs, pick=()):
    parts = len(refs)
    rows = src.shape[0] // (parts * PLANES)
    for a, ref in enumerate(refs):
        for m in range(PLANES):
            start = pl.multiple_of((me ^ (m * parts + a)) * rows, rows)
            ref[(m,) + pick] = src[pl.ds(start, rows), :].astype(ref.dtype)


def head_tiles(y, head):
    at = 256 * head
    qk, vt = y[:, at : at + 128], y[:, at + 128 : at + 256]
    low = lax.broadcasted_iota(jnp.int32, qk.shape, 1) < HD
    q = jnp.where(low, qk, 0.0).astype(bf16)
    k = jnp.where(low, pltpu.roll(qk, HD, 1), 0.0).astype(bf16)
    v = jnp.where(low, 0.0, pltpu.roll(vt, HD, 1)).astype(bf16)
    return q, k, v


def probs_of(q, k, tokens):
    s = nt(q, k) * (HD**-0.5)
    s = jnp.where(lax.broadcasted_iota(jnp.int32, s.shape, 1) < tokens, s, -1e30)
    e = jnp.exp(s - jnp.max(s, axis=-1, keepdims=True))
    return e / jnp.sum(e, axis=-1, keepdims=True)


def attn_fwd_kernel(tokens, parts, gain_row, first, scal, *refs):
    me, core = scal[0], scal[1]
    refs = list(refs)
    x_ref = refs.pop(0)
    if first:
        x = x_ref[...]
    else:
        own, other, rows_ref = refs.pop(0), refs.pop(0), refs.pop(0)
        x = x_ref[...] + join_halves(core, own[...], other[...])
    blocks = [refs.pop(0) for _ in range(parts)]
    if first:
        keep_ref, send_ref, rows_ref, w = refs
    else:
        x_out, keep_ref, send_ref, w = refs
    assemble(w, me, blocks)
    model = w.shape[0]
    if first:
        eye = (
            lax.broadcasted_iota(jnp.int32, (8, 128), 0)
            == lax.broadcasted_iota(jnp.int32, (8, 128), 1)
        ).astype(bf16)
        rows_ref[...] = nt(eye, w[:, model:].astype(bf16))
    else:
        x_out[...] = x
    hat, _ = norm_parts(x)
    h = (hat * rows_ref[gain_row : gain_row + 1, :]).astype(bf16)
    y = nn(h, w[:, :model].astype(bf16))
    branch = jnp.zeros(x.shape, f32)
    for head in range(model // 256):
        q, k, v = head_tiles(y, head)
        p = probs_of(q, k, tokens).astype(bf16)
        o = nn(p, v).astype(bf16)
        at = 256 * head + 128
        branch += nt(o, w[:, at : at + 128].astype(bf16))
    keep, send = split_halves(core, branch)
    keep_ref[...] = keep
    send_ref[...] = send.astype(send_ref.dtype)


def mlp_fwd_kernel(parts, gain_row, scal, x_ref, own, other, rows_ref, *refs):
    me, core = scal[0], scal[1]
    blocks, (x_out, keep_ref, send_ref, up, down) = refs[:parts], refs[parts:]
    assemble(up, me, blocks, (0,))
    assemble(down, me, blocks, (1,))
    x = x_ref[...] + join_halves(core, own[...], other[...])
    x_out[...] = x
    hat, _ = norm_parts(x)
    h = (hat * rows_ref[gain_row : gain_row + 1, :]).astype(bf16)
    u = nn(h, up[...].astype(bf16))
    r = (0.5 * u * (1.0 + lax.erf(u * root_half))).astype(bf16)
    keep, send = split_halves(core, nt(r, down[...].astype(bf16)))
    keep_ref[...] = keep
    send_ref[...] = send.astype(send_ref.dtype)


def router_probs(h, rows_ref):
    logits = nt(h, rows_ref[...].astype(bf16))
    lane = lax.broadcasted_iota(jnp.int32, logits.shape, 1)
    logits = jnp.where(lane < PLANES, logits, -1e30)
    e = jnp.exp(logits - jnp.max(logits, axis=-1, keepdims=True))
    return e / jnp.sum(e, axis=-1, keepdims=True), lane


def routed(routes, lane):
    return (routes[:, 0:1] == lane) | (routes[:, 1:2] == lane)


def moe_pre_kernel(tokens, gain_row, scal, x_ref, own, other, rows_ref, routes, x_out, h_out, half_out):
    core = scal[1]
    x = x_ref[...] + join_halves(core, own[...], other[...])
    x_out[...] = x
    hat, _ = norm_parts(x)
    h = (hat * rows_ref[gain_row : gain_row + 1, :]).astype(bf16)
    probs, lane = router_probs(h, rows_ref)
    gates = jnp.where(routed(routes[...], lane), probs, 0.0).astype(bf16)
    eye = (
        lax.broadcasted_iota(jnp.int32, (8, 8), 0) == lax.broadcasted_iota(jnp.int32, (8, 8), 1)
    ).astype(bf16)
    gate_rows = nt(eye, gates)
    padded, model = x.shape
    half = model // 2
    live = lax.broadcasted_iota(jnp.int32, x.shape, 0) < tokens
    h = jnp.where(live, h.astype(f32), 0.0)
    wide = jnp.concatenate([gate_rows, jnp.zeros((8, half - padded), f32)], axis=1)
    block = jnp.concatenate([jnp.zeros((padded - 8, half), f32), wide], axis=0)
    low, high = h[:, :half] + block, h[:, half:] + block
    h_out[...] = jnp.concatenate([low, high], axis=1).astype(bf16)
    half_out[...] = jnp.where(core == 0, low, high).astype(bf16)


def moe_kernel(parts, scal, *refs):
    me, core, expert = scal[0], scal[1], scal[2]
    refs = list(refs)
    h_refs = [refs.pop(0) for _ in range(1 + 2 * (PLANES - 1))]
    g_refs = [refs.pop(0) for _ in range(1 + 2 * (PLANES - 1))]
    blocks = [refs.pop(0) for _ in range(2 * parts)]
    y_keep, y_send, d_keep, d_send = [refs.pop(0) for _ in range(4)]
    grads = [refs.pop(0) for _ in range(2 * parts)]
    up, down, hs, gs, rs, dus, dys, acc = refs
    assemble(up, me, blocks[:parts])
    assemble(down, me, blocks[parts:])
    for dst, src in ((hs, h_refs), (gs, g_refs)):
        dst[0] = src[0][...]
        for m in range(1, PLANES):
            dst[m] = join_halves(core, src[m][...], src[PLANES - 1 + m][...])
    padded, model = hs.shape[1:]
    half = model // 2

    def step(m, carry):
        h, g = hs[m], gs[m]
        rows = h.astype(f32)[padded - 8 :, :256]
        pick = row_of(expert, (8, 128)).astype(f32)
        gate = tn(rows, pick)[:padded, :1]
        u = nn(h, up[...].astype(bf16))
        cdf = 0.5 * (1.0 + lax.erf(u * root_half))
        r = (u * cdf).astype(bf16)
        t = nn(g, down[...].astype(bf16))
        slope = cdf + u * inv_root_two_pi * jnp.exp(-0.5 * u * u)
        du = (gate * t * slope).astype(bf16)
        rs[m] = r
        dus[m] = du
        dys[m] = (gate * g.astype(f32)).astype(bf16)
        dots = nt(jnp.ones((8, r.shape[1]), bf16), (r.astype(f32) * t).astype(bf16))
        dots = jnp.where(row_of(expert, dots.shape), dots, 0.0)
        y = gate * nt(r, down[...].astype(bf16))
        keep, send = split_halves(core, y)
        y_keep[m] = keep
        y_send[m] = send.astype(y_send.dtype)
        dh = nt(du, up[...].astype(bf16))
        wide = jnp.concatenate([dots, jnp.zeros((8, model - padded), f32)], axis=1)
        dh = dh + jnp.concatenate([jnp.zeros((padded - 8, model), f32), wide], axis=0)
        keep, send = split_halves(core, dh)
        d_keep[m] = keep
        d_send[m] = send.astype(d_send.dtype)
        return carry

    lax.fori_loop(0, PLANES, step, 0)
    flat = (PLANES * padded, model)
    acc[...] = tn(hs[...].reshape(flat), dus[...].reshape(flat)).astype(acc.dtype)
    scatter_blocks(acc, me, grads[:parts])
    acc[...] = tn(dys[...].reshape(flat), rs[...].reshape(flat)).astype(acc.dtype)
    scatter_blocks(acc, me, grads[parts:])


def plain_pull(x_ref, own, other, g_ref, rows_ref, small_ref, gain_row, core):
    dh = join_halves(core, own[...], other[...])
    dx, dgain = norm_pull(x_ref[...], rows_ref[gain_row : gain_row + 1, :], dh)
    small = small_ref[...] + jnp.where(row_of(gain_row, small_ref.shape), dgain, 0.0)
    return g_ref[...] + dx, small


def router_pull(tokens, x_ref, own, other, g_ref, rows_ref, routes, gain_row, core):
    dh = join_halves(core, own[...], other[...])
    padded, model = dh.shape
    gain = rows_ref[gain_row : gain_row + 1, :]
    hat, _ = norm_parts(x_ref[...])
    live = lax.broadcasted_iota(jnp.int32, dh.shape, 0) < tokens
    h = (hat * gain).astype(bf16)
    probs, lane = router_probs(h, rows_ref)
    dots = dh[padded - 8 :, :256]
    eye = (
        lax.broadcasted_iota(jnp.int32, (8, 8), 0) == lax.broadcasted_iota(jnp.int32, (8, 8), 1)
    ).astype(f32)
    dprobs = lax.dot_general(
        dots, eye, (((0,), (0,)), ((), ())), precision=highest, preferred_element_type=f32
    )[:padded]
    keep = routed(routes[...], lane) & (lax.broadcasted_iota(jnp.int32, lane.shape, 0) < tokens)
    dprobs = jnp.where(keep, dprobs, 0.0)
    dlogits = probs * (dprobs - jnp.sum(probs * dprobs, axis=-1, keepdims=True))
    small = lax.dot_general(
        dlogits, h.astype(f32), (((0,), (0,)), ((), ())), precision=highest, preferred_element_type=f32
    )
    router = jnp.where(lax.broadcasted_iota(jnp.int32, small.shape, 0) < PLANES, rows_ref[...], 0.0)
    dh = jnp.where(live, dh, 0.0) + lax.dot_general(
        dlogits, router, (((1,), (0,)), ((), ())), precision=highest, preferred_element_type=f32
    )
    dx, dgain = norm_pull(x_ref[...], gain, dh)
    small = small + jnp.where(row_of(gain_row, small.shape), dgain, 0.0)
    return g_ref[...] + dx, small


def attn_bwd_kernel(tokens, parts, rows_at, last, scal, *refs):
    me, core = scal[0], scal[1]
    refs = list(refs)
    x_up, own, other, g_ref, rows_ref, extra, x_ref = [refs.pop(0) for _ in range(7)]
    blocks = [refs.pop(0) for _ in range(parts)]
    g_out, small_out, keep_ref, send_ref = [refs.pop(0) for _ in range(4)]
    grads = [refs.pop(0) for _ in range(parts)]
    w, acc = refs
    assemble(w, me, blocks)
    up_row, gain_row = rows_at
    if last:
        g, small = plain_pull(x_up, own, other, g_ref, rows_ref, extra, up_row, core)
    else:
        g, small = router_pull(tokens, x_up, own, other, g_ref, rows_ref, extra, up_row, core)
    g_out[...] = g
    small_out[...] = small
    model = acc.shape[1]
    hat, _ = norm_parts(x_ref[...])
    h = (hat * rows_ref[gain_row : gain_row + 1, :]).astype(bf16)
    db = g.astype(bf16)
    y = nn(h, w[:, :model].astype(bf16))
    dh = jnp.zeros(g.shape, f32)
    left, right = [], []
    for head in range(model // 256):
        at = 256 * head
        q, k, v = head_tiles(y, head)
        p = probs_of(q, k, tokens)
        pb = p.astype(bf16)
        o = nn(pb, v).astype(bf16)
        wqk = w[:, at : at + 128].astype(bf16)
        wvo = w[:, at + 128 : at + 256].astype(bf16)
        do = nn(db, wvo)
        low = lax.broadcasted_iota(jnp.int32, do.shape, 1) < HD
        do = jnp.where(low, 0.0, do).astype(bf16)
        dp = nt(do, v)
        dv = tn(pb, do)
        ds = (p * (dp - jnp.sum(p * dp, axis=-1, keepdims=True))).astype(bf16)
        dq = nn(ds, k) * (HD**-0.5)
        dk = tn(ds, q) * (HD**-0.5)
        dqk = (dq + pltpu.roll(dk, HD, 1)).astype(bf16)
        dvt = pltpu.roll(dv, HD, 1).astype(bf16)
        dh += nt(dqk, wqk) + nt(dvt, wvo)
        left += [dqk, dvt]
        right += [jnp.zeros_like(o), o]
    keep, send = split_halves(core, dh)
    keep_ref[...] = keep
    send_ref[...] = send.astype(send_ref.dtype)
    grad = tn(h, jnp.concatenate(left, axis=1)) + tn(db, jnp.concatenate(right, axis=1))
    acc[...] = grad.astype(acc.dtype)
    scatter_blocks(acc, me, grads)


def mlp_bwd_kernel(parts, rows_at, scal, x_up, own, other, g_ref, rows_ref, extra, x_ref, *refs):
    me, core = scal[0], scal[1]
    refs = list(refs)
    blocks = [refs.pop(0) for _ in range(parts)]
    g_out, small_out, keep_ref, send_ref = [refs.pop(0) for _ in range(4)]
    grads = [refs.pop(0) for _ in range(parts)]
    up, down, acc = refs
    assemble(up, me, blocks, (0,))
    assemble(down, me, blocks, (1,))
    up_row, gain_row = rows_at
    g, small = plain_pull(x_up, own, other, g_ref, rows_ref, extra, up_row, core)
    g_out[...] = g
    small_out[...] = small
    hat, _ = norm_parts(x_ref[...])
    h = (hat * rows_ref[gain_row : gain_row + 1, :]).astype(bf16)
    dm = g.astype(bf16)
    u = nn(h, up[...].astype(bf16))
    cdf = 0.5 * (1.0 + lax.erf(u * root_half))
    r = (u * cdf).astype(bf16)
    slope = cdf + u * inv_root_two_pi * jnp.exp(-0.5 * u * u)
    du = (nn(dm, down[...].astype(bf16)) * slope).astype(bf16)
    keep, send = split_halves(core, nt(du, up[...].astype(bf16)))
    keep_ref[...] = keep
    send_ref[...] = send.astype(send_ref.dtype)
    acc[...] = tn(h, du).astype(acc.dtype)
    scatter_blocks(acc, me, grads, (0,))
    acc[...] = tn(dm, r).astype(acc.dtype)
    scatter_blocks(acc, me, grads, (1,))


def final_kernel(tokens, gain_row, scal, x_ref, own, other, g_ref, rows_ref, extra, g_out, *refs):
    me, core = scal[0], scal[1]
    grads, acc = refs[:-1], refs[-1]
    g, small = plain_pull(x_ref, own, other, g_ref, rows_ref, extra, gain_row, core)
    g_out[...] = g[:tokens]
    eye = (
        lax.broadcasted_iota(jnp.int32, (8, 128), 0) == lax.broadcasted_iota(jnp.int32, (8, 128), 1)
    ).astype(f32)
    acc[...] = lax.dot_general(
        small, eye, (((0,), (0,)), ((), ())), precision=highest, preferred_element_type=f32
    )
    scatter_blocks(acc, me, grads)


def run(kernel, scal, ins, outs, scratch, flops, vmem_mib=24):
    vmem = pl.BlockSpec(memory_space=pltpu.VMEM)
    size = lambda s: s.size * s.dtype.itemsize
    return pl.pallas_call(
        kernel,
        out_shape=outs,
        in_specs=[pl.BlockSpec(memory_space=pltpu.SMEM)] + [vmem] * len(ins),
        out_specs=[vmem] * len(outs),
        scratch_shapes=scratch,
        compiler_params=pltpu.CompilerParams(vmem_limit_bytes=vmem_mib * 2**20),
        cost_estimate=pl.CostEstimate(
            flops=int(flops),
            bytes_accessed=int(sum(size(a) for a in ins) + sum(size(o) for o in outs)),
            transcendentals=0,
        ),
    )(scal, *ins)


def shape(dims, kind):
    return jax.ShapeDtypeStruct(tuple(dims), kind)


def tie(value, *after):
    return lax.optimization_barrier((value,) + after)[0]


def bar(*values):
    return lax.optimization_barrier(values)


def shards(
    fsdp,
    tensor,
    activations,
    image_live,
    expert_routes,
    attn_gain_one,
    qkv_weight_one,
    out_weight_one,
    first_feedforward_gain,
    up_weight_one,
    down_weight_one,
    attn_gain_two,
    qkv_weight_two,
    out_weight_two,
    moe_gain_two,
    router_weight,
    expert_up,
    expert_down,
    cotangent,
):
    parts = fsdp // PLANES
    tokens, model = activations.shape[1:]
    padded = -(-(tokens + 8) // 16) * 16
    half = model // 2
    rows = model // fsdp
    heads = qkv_weight_one.shape[2] // HD
    hidden = up_weight_one.shape[1]
    held = bf16 if rows % 16 == 0 else f32
    me = lax.axis_index("fsdp")
    place = lax.axis_index("tensor")
    core, plane = place % 2, me // parts
    scal = jnp.stack([me, core, plane, place]).astype(jnp.int32)

    def across(value, k):
        return lax.ppermute(value, "fsdp", [(i, i ^ k) for i in range(fsdp)])

    def over(value, k):
        return lax.ppermute(value, "tensor", [(i, i ^ k) for i in range(tensor)])

    def spread(stacked):
        arrays, bit = [stacked], 1
        while bit < parts:
            arrays += [across(a, bit) for a in arrays]
            bit *= 2
        return arrays

    def gather_planes(block):
        return jnp.stack([block] + [across(block, m * parts) for m in range(1, PLANES)])

    def planes(blocks):
        return [blocks[0]] + [across(blocks[m].astype(bf16), m * parts) for m in range(1, PLANES)]

    def added(arrays):
        return sum([a.astype(f32) for a in arrays[1:]], arrays[0].astype(f32))

    def enclosed(stage, *operands):
        def idle(*args):
            return jax.tree.map(lambda r: jnp.zeros(r.shape, r.dtype), jax.eval_shape(stage, *args))

        return lax.cond(me < fsdp, stage, idle, *operands)

    def fold(arrays):
        arrays, bit = list(arrays), parts // 2
        while bit:
            for a in range(bit):
                arrays[a] = arrays[a].astype(f32) + across(arrays[a + bit].astype(bf16), bit).astype(f32)
            bit //= 2
        return arrays[0]

    def reduce_planes(stacked):
        total = stacked[0].astype(f32)
        for m in range(1, PLANES):
            total = total + across(stacked[m].astype(bf16), m * parts).astype(f32)
        return total

    def pair(total):
        low = total.astype(bf16)
        total = low.astype(f32) + over(low, 2).astype(f32)
        return total, over(total, 1)

    def joined(keep, send):
        return pair(keep + over(send, 1))

    def attn_pack(qkv, out):
        by_head = jnp.moveaxis(qkv.reshape(3, rows, heads, HD), 0, 2)
        out = out.reshape(heads, HD, rows).transpose(2, 0, 1)[:, :, None]
        return jnp.concatenate([by_head, out], axis=2).reshape(rows, heads * 4 * HD)

    def attn_unpack(grad):
        grad = grad.reshape(rows, heads, 4, HD)
        qkv = jnp.moveaxis(grad[:, :, :3], 2, 0).reshape(3, rows, heads * HD)
        return qkv, grad[:, :, 3].transpose(1, 2, 0).reshape(heads * HD, rows)

    smalls = jnp.concatenate(
        [
            router_weight,
            attn_gain_one[:, None],
            first_feedforward_gain[:, None],
            attn_gain_two[:, None],
            moe_gain_two[:, None],
        ],
        axis=1,
    )
    smalls = jnp.pad(smalls, ((0, 0), (0, 128 - smalls.shape[1])))
    one = jnp.concatenate([attn_pack(qkv_weight_one, out_weight_one), smalls], axis=1)
    one = gather_planes(one)
    w_one = spread(one)
    mlp = jnp.stack([up_weight_one, down_weight_one.T])
    mlp = gather_planes(tie(mlp, one))
    w_mlp = spread(mlp)
    two = gather_planes(tie(attn_pack(qkv_weight_two, out_weight_two), mlp))

    def by_plane(experts):
        return [lax.dynamic_index_in_dim(experts, plane ^ m, 0, keepdims=False) for m in range(PLANES)]

    e_up = planes(tie(by_plane(expert_up), two))
    e_down = by_plane(jnp.swapaxes(expert_down, 1, 2))

    pad = ((0, padded - tokens), (0, 0))
    stream0 = jnp.pad(activations[0], pad)
    grad3 = jnp.pad(cotangent[0] * image_live[0].astype(f32), pad)
    routes = jnp.pad(expert_routes[0], pad, constant_values=-1)
    grad_low = grad3.astype(bf16)
    grad_half = jnp.where(core == 0, grad_low[:, :half], grad_low[:, half:])

    stream = shape((padded, model), f32)
    pieces = [shape((padded, half), f32)] * 2
    wide = pltpu.VMEM((model, model + 128), held)
    square = pltpu.VMEM((model, model), held)
    unit = 2 * padded * model * model

    keep, send, small_rows = run(
        functools.partial(attn_fwd_kernel, tokens, parts, 4, True),
        scal,
        [stream0] + w_one,
        pieces + [shape((8, model), f32)],
        [wide],
        3 * unit,
    )
    own, other = joined(keep, send)
    own, other, two, e_up, e_down = bar(own, other, two, e_up, e_down)
    w_two, e_down = spread(two), planes(e_down)

    def stage_two(scal, *ins):
        stream1, keep, send = run(
            functools.partial(mlp_fwd_kernel, parts, 5),
            scal,
            ins,
            [stream] + pieces,
            [square, square],
            2 * unit,
        )
        return stream1, *joined(keep, send)

    stream1, own, other = enclosed(stage_two, scal, stream0, own, other, small_rows, *w_mlp)
    own, other, w_two, e_down, grad_half = bar(own, other, w_two, e_down, grad_half)
    w_e_up = spread(jnp.stack(e_up))
    g_near = planes([grad_half] * PLANES)[1:]

    def stage_three(scal, routes, small_rows, *ins):
        stream2, keep, send = run(
            functools.partial(attn_fwd_kernel, tokens, parts, 6, False),
            scal,
            [*ins[:3], small_rows, *ins[3:]],
            [stream] + pieces,
            [square],
            3 * unit,
        )
        outs = run(
            functools.partial(moe_pre_kernel, tokens, 7),
            scal,
            [stream2, *joined(keep, send), small_rows, routes],
            [stream, shape((padded, model), bf16), shape((padded, half), bf16)],
            [],
            unit / 50,
        )
        return stream2, *outs

    stream2, stream3, h_full, h_half = enclosed(
        stage_three, scal, routes, small_rows, stream1, own, other, *w_two
    )
    h_half, w_e_up, g_near = bar(h_half, w_e_up, g_near)
    h_near = planes([h_half] * PLANES)[1:]
    w_moe = w_e_up + spread(jnp.stack(e_down))
    h_blocks = [h_full] + h_near + [over(n, 1) for n in h_near]
    g_blocks = [grad_low] + g_near + [over(n, 1) for n in g_near]
    images = pltpu.VMEM((PLANES, padded, model), bf16)
    image_hidden = pltpu.VMEM((PLANES, padded, hidden), bf16)
    block_pieces = [shape((PLANES, padded, half), f32), shape((PLANES, padded, half), bf16)]
    y_keep, y_send, d_keep, d_send, *expert_grads = run(
        functools.partial(moe_kernel, parts),
        scal,
        h_blocks + g_blocks + w_moe,
        block_pieces * 2 + [shape((PLANES, rows, hidden), bf16)] * (2 * parts),
        [square, square, images, images, image_hidden, image_hidden, images, square],
        24 * unit,
        40,
    )

    def home(keep, send):
        summed = keep + over(send, 1).astype(f32)
        return planes(list(summed))

    block_grads = [shape((PLANES, rows, model), bf16)] * parts
    own, other = pair(added(home(d_keep, d_send)))
    e_up, e_down = fold(expert_grads[:parts]), fold(expert_grads[parts:])
    own, other, e_up = bar(own, other, e_up)
    e_up = planes(list(e_up))
    grad2, small, keep, send, *two_sum = run(
        functools.partial(attn_bwd_kernel, tokens, parts, (7, 6), False),
        scal,
        [stream3, own, other, grad3, small_rows, routes, stream2] + w_two,
        [stream, shape((8, model), f32)] + pieces + block_grads,
        [square, square],
        8 * unit,
    )
    keep, send, e_up, e_down = bar(keep, send, e_up, e_down)
    e_down = planes(list(e_down))
    two_sum = fold(two_sum)
    own, other = joined(keep, send)
    own, other, e_down, two_sum = bar(own, other, e_down, two_sum)
    grad1, small, keep, send, *mlp_sum = run(
        functools.partial(mlp_bwd_kernel, parts, (6, 5)),
        scal,
        [stream2, own, other, grad2, small_rows, small, stream1] + w_mlp,
        [stream, shape((8, model), f32)]
        + pieces
        + [shape((PLANES, 2, rows, hidden), bf16)] * parts,
        [square, square, square],
        5 * unit,
    )
    mlp_sum = fold(mlp_sum)
    two_sum = planes(list(two_sum))
    own, other = joined(keep, send)
    y_keep, y_send = bar(y_keep, y_send, keep)[:2]
    y_own = home(y_keep, y_send)
    own, other, mlp_sum, two_sum, y_own = bar(own, other, mlp_sum, two_sum, y_own)
    mlp_sum = planes(list(mlp_sum))
    y_own, y_other = pair(added(y_own))
    grad0, small, keep, send, *one_sum = run(
        functools.partial(attn_bwd_kernel, tokens, parts, (5, 4), True),
        scal,
        [stream1, own, other, grad1, small_rows, small, stream0] + w_one,
        [stream, shape((8, model), f32)] + pieces + block_grads,
        [wide, square],
        8 * unit,
    )
    one_sum = fold(one_sum)
    own, other = joined(keep, send)
    own, other, one_sum, mlp_sum = bar(own, other, one_sum, mlp_sum)
    one_sum = planes(list(one_sum))
    input_grad, *small_grads = run(
        functools.partial(final_kernel, tokens, 4),
        scal,
        [stream0, own, other, grad0, small_rows, small],
        [shape((tokens, model), f32)] + [shape((PLANES, rows, 128), bf16)] * parts,
        [pltpu.VMEM((model, 128), f32)],
        unit / 50,
    )
    small_sum = reduce_planes(fold(small_grads))
    one_sum, two_sum, mlp_sum = added(one_sum), added(two_sum), added(mlp_sum)

    low = jnp.where(core == 0, y_own, y_other)
    high = jnp.where(core == 0, y_other, y_own)
    result = (stream3 + jnp.concatenate([low, high], axis=1))[:tokens]

    bit0, bit1 = plane % 2 == 1, plane // 2 == 1

    def of_expert(came, x):
        a, b = jnp.where(bit0, came[x ^ 1], came[x]), jnp.where(bit0, came[x ^ 3], came[x ^ 2])
        return jnp.where(bit1, b, a).astype(f32)

    grad_up = jnp.stack([of_expert(e_up, x) for x in range(PLANES)])
    grad_down = jnp.stack([of_expert(e_down, x).T for x in range(PLANES)])
    qkv_one, out_one = attn_unpack(one_sum)
    qkv_two, out_two = attn_unpack(two_sum)
    return (
        result[None],
        input_grad[None],
        small_sum[:, 4],
        qkv_one,
        out_one,
        small_sum[:, 5],
        mlp_sum[0],
        mlp_sum[1].T,
        small_sum[:, 6],
        qkv_two,
        out_two,
        small_sum[:, 7],
        small_sum[:, :PLANES],
        grad_up,
        grad_down,
    )


def solution(mesh):
    return jax.shard_map(
        functools.partial(shards, mesh.shape["fsdp"], mesh.shape["tensor"]),
        mesh=mesh,
        in_specs=(
            P("fsdp", None, None),
            P("fsdp"),
            P("fsdp", None, None),
            P("fsdp"),
            P(None, "fsdp", "tensor"),
            P("tensor", "fsdp"),
            P("fsdp"),
            P("fsdp", "tensor"),
            P("tensor", "fsdp"),
            P("fsdp"),
            P(None, "fsdp", "tensor"),
            P("tensor", "fsdp"),
            P("fsdp"),
            P("fsdp", None),
            P(None, "fsdp", "tensor"),
            P(None, "tensor", "fsdp"),
            P("fsdp", None, None),
        ),
        out_specs=(
            P("fsdp", None, None),
            P("fsdp", None, None),
            P("fsdp"),
            P(None, "fsdp", "tensor"),
            P("tensor", "fsdp"),
            P("fsdp"),
            P("fsdp", "tensor"),
            P("tensor", "fsdp"),
            P("fsdp"),
            P(None, "fsdp", "tensor"),
            P("tensor", "fsdp"),
            P("fsdp"),
            P("fsdp", None),
            P(None, "fsdp", "tensor"),
            P(None, "tensor", "fsdp"),
        ),
        check_vma=False,
    )
```

```python
import functools

import jax
import jax.numpy as jnp
from jax import lax
from jax.experimental import pallas as pl
from jax.experimental.pallas import tpu as pltpu
from jax.sharding import PartitionSpec as P

HD = 64
PLANES = 4
epsilon = 1e-06
root_half = 0.7071067811865476
inv_root_two_pi = 0.3989422804014327
highest = lax.Precision.HIGHEST
bf16 = jnp.bfloat16
f32 = jnp.float32


def nn(a, b):
    return lax.dot_general(a, b, (((1,), (0,)), ((), ())), preferred_element_type=f32)


def nt(a, b):
    return lax.dot_general(a, b, (((1,), (1,)), ((), ())), preferred_element_type=f32)


def tn(a, b):
    return lax.dot_general(a, b, (((0,), (0,)), ((), ())), preferred_element_type=f32)


def norm_parts(x):
    c = x - jnp.mean(x, axis=-1, keepdims=True)
    rs = lax.rsqrt(jnp.mean(c * c, axis=-1, keepdims=True) + epsilon)
    return c * rs, rs


def norm_pull(x, gain, dh):
    hat, rs = norm_parts(x)
    t = dh * gain
    mean_t = jnp.mean(t, axis=-1, keepdims=True)
    mean_th = jnp.mean(t * hat, axis=-1, keepdims=True)
    return rs * (t - mean_t - hat * mean_th), jnp.sum(dh * hat, axis=0, keepdims=True)


def join_halves(core, own, other):
    low = jnp.where(core == 0, own, other)
    high = jnp.where(core == 0, other, own)
    return jnp.concatenate([low, high], axis=1)


def split_halves(core, full):
    half = full.shape[1] // 2
    low, high = full[:, :half], full[:, half:]
    return jnp.where(core == 0, low, high), jnp.where(core == 0, high, low)


def row_of(index, shape):
    return lax.broadcasted_iota(jnp.int32, shape, 0) == index


def assemble(dst, me, refs, pick=()):
    parts = len(refs)
    rows = dst.shape[0] // (parts * PLANES)
    for a, ref in enumerate(refs):
        for m in range(PLANES):
            start = pl.multiple_of((me ^ (m * parts + a)) * rows, rows)
            dst[pl.ds(start, rows), :] = ref[(m,) + pick].astype(dst.dtype)


def scatter_blocks(src, me, refs, pick=()):
    parts = len(refs)
    rows = src.shape[0] // (parts * PLANES)
    for a, ref in enumerate(refs):
        for m in range(PLANES):
            start = pl.multiple_of((me ^ (m * parts + a)) * rows, rows)
            ref[(m,) + pick] = src[pl.ds(start, rows), :].astype(ref.dtype)


def head_tiles(y, head):
    at = 256 * head
    qk, vt = y[:, at : at + 128], y[:, at + 128 : at + 256]
    low = lax.broadcasted_iota(jnp.int32, qk.shape, 1) < HD
    q = jnp.where(low, qk, 0.0).astype(bf16)
    k = jnp.where(low, pltpu.roll(qk, HD, 1), 0.0).astype(bf16)
    v = jnp.where(low, 0.0, pltpu.roll(vt, HD, 1)).astype(bf16)
    return q, k, v


def probs_of(q, k, tokens):
    s = nt(q, k) * (HD**-0.5)
    s = jnp.where(lax.broadcasted_iota(jnp.int32, s.shape, 1) < tokens, s, -1e30)
    e = jnp.exp(s - jnp.max(s, axis=-1, keepdims=True))
    return e / jnp.sum(e, axis=-1, keepdims=True)


def attn_fwd_kernel(tokens, parts, gain_row, first, scal, *refs):
    me, core = scal[0], scal[1]
    refs = list(refs)
    x_ref = refs.pop(0)
    if first:
        x = x_ref[...]
    else:
        own, other, rows_ref = refs.pop(0), refs.pop(0), refs.pop(0)
        x = x_ref[...] + join_halves(core, own[...], other[...])
    blocks = [refs.pop(0) for _ in range(parts)]
    if first:
        keep_ref, send_ref, rows_ref, w = refs
    else:
        x_out, keep_ref, send_ref, w = refs
    assemble(w, me, blocks)
    model = w.shape[0]
    if first:
        eye = (
            lax.broadcasted_iota(jnp.int32, (8, 128), 0)
            == lax.broadcasted_iota(jnp.int32, (8, 128), 1)
        ).astype(bf16)
        rows_ref[...] = nt(eye, w[:, model:].astype(bf16))
    else:
        x_out[...] = x
    hat, _ = norm_parts(x)
    h = (hat * rows_ref[gain_row : gain_row + 1, :]).astype(bf16)
    y = nn(h, w[:, :model].astype(bf16))
    branch = jnp.zeros(x.shape, f32)
    for head in range(model // 256):
        q, k, v = head_tiles(y, head)
        p = probs_of(q, k, tokens).astype(bf16)
        o = nn(p, v).astype(bf16)
        at = 256 * head + 128
        branch += nt(o, w[:, at : at + 128].astype(bf16))
    keep, send = split_halves(core, branch)
    keep_ref[...] = keep
    send_ref[...] = send.astype(send_ref.dtype)


def mlp_fwd_kernel(parts, gain_row, scal, x_ref, own, other, rows_ref, *refs):
    me, core = scal[0], scal[1]
    blocks, (x_out, keep_ref, send_ref, up, down) = refs[:parts], refs[parts:]
    assemble(up, me, blocks, (0,))
    assemble(down, me, blocks, (1,))
    x = x_ref[...] + join_halves(core, own[...], other[...])
    x_out[...] = x
    hat, _ = norm_parts(x)
    h = (hat * rows_ref[gain_row : gain_row + 1, :]).astype(bf16)
    u = nn(h, up[...].astype(bf16))
    r = (0.5 * u * (1.0 + lax.erf(u * root_half))).astype(bf16)
    keep, send = split_halves(core, nt(r, down[...].astype(bf16)))
    keep_ref[...] = keep
    send_ref[...] = send.astype(send_ref.dtype)


def router_probs(h, rows_ref):
    logits = nt(h, rows_ref[...].astype(bf16))
    lane = lax.broadcasted_iota(jnp.int32, logits.shape, 1)
    logits = jnp.where(lane < PLANES, logits, -1e30)
    e = jnp.exp(logits - jnp.max(logits, axis=-1, keepdims=True))
    return e / jnp.sum(e, axis=-1, keepdims=True), lane


def routed(routes, lane):
    return (routes[:, 0:1] == lane) | (routes[:, 1:2] == lane)


def moe_pre_kernel(tokens, gain_row, scal, x_ref, own, other, rows_ref, routes, x_out, h_out, half_out):
    core = scal[1]
    x = x_ref[...] + join_halves(core, own[...], other[...])
    x_out[...] = x
    hat, _ = norm_parts(x)
    h = (hat * rows_ref[gain_row : gain_row + 1, :]).astype(bf16)
    probs, lane = router_probs(h, rows_ref)
    gates = jnp.where(routed(routes[...], lane), probs, 0.0).astype(bf16)
    eye = (
        lax.broadcasted_iota(jnp.int32, (8, 8), 0) == lax.broadcasted_iota(jnp.int32, (8, 8), 1)
    ).astype(bf16)
    gate_rows = nt(eye, gates)
    padded, model = x.shape
    half = model // 2
    live = lax.broadcasted_iota(jnp.int32, x.shape, 0) < tokens
    h = jnp.where(live, h.astype(f32), 0.0)
    wide = jnp.concatenate([gate_rows, jnp.zeros((8, half - padded), f32)], axis=1)
    block = jnp.concatenate([jnp.zeros((padded - 8, half), f32), wide], axis=0)
    low, high = h[:, :half] + block, h[:, half:] + block
    h_out[...] = jnp.concatenate([low, high], axis=1).astype(bf16)
    half_out[...] = jnp.where(core == 0, low, high).astype(bf16)


def moe_kernel(parts, scal, *refs):
    me, core, expert = scal[0], scal[1], scal[2]
    refs = list(refs)
    h_refs = [refs.pop(0) for _ in range(1 + 2 * (PLANES - 1))]
    g_refs = [refs.pop(0) for _ in range(1 + 2 * (PLANES - 1))]
    blocks = [refs.pop(0) for _ in range(2 * parts)]
    y_keep, y_send, d_keep, d_send = [refs.pop(0) for _ in range(4)]
    grads = [refs.pop(0) for _ in range(2 * parts)]
    up, down, hs, gs, rs, dus, dys, acc = refs
    assemble(up, me, blocks[:parts])
    assemble(down, me, blocks[parts:])
    for dst, src in ((hs, h_refs), (gs, g_refs)):
        dst[0] = src[0][...]
        for m in range(1, PLANES):
            dst[m] = join_halves(core, src[m][...], src[PLANES - 1 + m][...])
    padded, model = hs.shape[1:]
    half = model // 2

    def step(m, carry):
        h, g = hs[m], gs[m]
        rows = h.astype(f32)[padded - 8 :, :256]
        pick = row_of(expert, (8, 128)).astype(f32)
        gate = tn(rows, pick)[:padded, :1]
        u = nn(h, up[...].astype(bf16))
        cdf = 0.5 * (1.0 + lax.erf(u * root_half))
        r = (u * cdf).astype(bf16)
        t = nn(g, down[...].astype(bf16))
        slope = cdf + u * inv_root_two_pi * jnp.exp(-0.5 * u * u)
        du = (gate * t * slope).astype(bf16)
        rs[m] = r
        dus[m] = du
        dys[m] = (gate * g.astype(f32)).astype(bf16)
        dots = nt(jnp.ones((8, r.shape[1]), bf16), (r.astype(f32) * t).astype(bf16))
        dots = jnp.where(row_of(expert, dots.shape), dots, 0.0)
        y = gate * nt(r, down[...].astype(bf16))
        keep, send = split_halves(core, y)
        y_keep[m] = keep
        y_send[m] = send.astype(y_send.dtype)
        dh = nt(du, up[...].astype(bf16))
        wide = jnp.concatenate([dots, jnp.zeros((8, model - padded), f32)], axis=1)
        dh = dh + jnp.concatenate([jnp.zeros((padded - 8, model), f32), wide], axis=0)
        keep, send = split_halves(core, dh)
        d_keep[m] = keep
        d_send[m] = send.astype(d_send.dtype)
        return carry

    lax.fori_loop(0, PLANES, step, 0)
    flat = (PLANES * padded, model)
    acc[...] = tn(hs[...].reshape(flat), dus[...].reshape(flat)).astype(acc.dtype)
    scatter_blocks(acc, me, grads[:parts])
    acc[...] = tn(dys[...].reshape(flat), rs[...].reshape(flat)).astype(acc.dtype)
    scatter_blocks(acc, me, grads[parts:])


def plain_pull(x_ref, own, other, g_ref, rows_ref, small_ref, gain_row, core):
    dh = join_halves(core, own[...], other[...]).astype(f32)
    dx, dgain = norm_pull(x_ref[...], rows_ref[gain_row : gain_row + 1, :], dh)
    small = small_ref[...] + jnp.where(row_of(gain_row, small_ref.shape), dgain, 0.0)
    return g_ref[...] + dx, small


def router_pull(tokens, x_ref, own, other, g_ref, rows_ref, routes, gain_row, core):
    dh = join_halves(core, own[...], other[...]).astype(f32)
    padded, model = dh.shape
    gain = rows_ref[gain_row : gain_row + 1, :]
    hat, _ = norm_parts(x_ref[...])
    live = lax.broadcasted_iota(jnp.int32, dh.shape, 0) < tokens
    h = (hat * gain).astype(bf16)
    probs, lane = router_probs(h, rows_ref)
    dots = dh[padded - 8 :, :256]
    eye = (
        lax.broadcasted_iota(jnp.int32, (8, 8), 0) == lax.broadcasted_iota(jnp.int32, (8, 8), 1)
    ).astype(f32)
    dprobs = lax.dot_general(
        dots, eye, (((0,), (0,)), ((), ())), precision=highest, preferred_element_type=f32
    )[:padded]
    keep = routed(routes[...], lane) & (lax.broadcasted_iota(jnp.int32, lane.shape, 0) < tokens)
    dprobs = jnp.where(keep, dprobs, 0.0)
    dlogits = probs * (dprobs - jnp.sum(probs * dprobs, axis=-1, keepdims=True))
    small = lax.dot_general(
        dlogits, h.astype(f32), (((0,), (0,)), ((), ())), precision=highest, preferred_element_type=f32
    )
    router = jnp.where(lax.broadcasted_iota(jnp.int32, small.shape, 0) < PLANES, rows_ref[...], 0.0)
    dh = jnp.where(live, dh, 0.0) + lax.dot_general(
        dlogits, router, (((1,), (0,)), ((), ())), precision=highest, preferred_element_type=f32
    )
    dx, dgain = norm_pull(x_ref[...], gain, dh)
    small = small + jnp.where(row_of(gain_row, small.shape), dgain, 0.0)
    return g_ref[...] + dx, small


def attn_bwd_kernel(tokens, parts, rows_at, last, scal, *refs):
    me, core = scal[0], scal[1]
    refs = list(refs)
    x_up, own, other, g_ref, rows_ref, extra, x_ref = [refs.pop(0) for _ in range(7)]
    blocks = [refs.pop(0) for _ in range(parts)]
    g_out, small_out, keep_ref, send_ref = [refs.pop(0) for _ in range(4)]
    grads = [refs.pop(0) for _ in range(parts)]
    w, acc = refs
    assemble(w, me, blocks)
    up_row, gain_row = rows_at
    if last:
        g, small = plain_pull(x_up, own, other, g_ref, rows_ref, extra, up_row, core)
    else:
        g, small = router_pull(tokens, x_up, own, other, g_ref, rows_ref, extra, up_row, core)
    g_out[...] = g
    small_out[...] = small
    model = acc.shape[1]
    hat, _ = norm_parts(x_ref[...])
    h = (hat * rows_ref[gain_row : gain_row + 1, :]).astype(bf16)
    db = g.astype(bf16)
    y = nn(h, w[:, :model].astype(bf16))
    dh = jnp.zeros(g.shape, f32)
    left, right = [], []
    for head in range(model // 256):
        at = 256 * head
        q, k, v = head_tiles(y, head)
        p = probs_of(q, k, tokens)
        pb = p.astype(bf16)
        o = nn(pb, v).astype(bf16)
        wqk = w[:, at : at + 128].astype(bf16)
        wvo = w[:, at + 128 : at + 256].astype(bf16)
        do = nn(db, wvo)
        low = lax.broadcasted_iota(jnp.int32, do.shape, 1) < HD
        do = jnp.where(low, 0.0, do).astype(bf16)
        dp = nt(do, v)
        dv = tn(pb, do)
        ds = (p * (dp - jnp.sum(p * dp, axis=-1, keepdims=True))).astype(bf16)
        dq = nn(ds, k) * (HD**-0.5)
        dk = tn(ds, q) * (HD**-0.5)
        dqk = (dq + pltpu.roll(dk, HD, 1)).astype(bf16)
        dvt = pltpu.roll(dv, HD, 1).astype(bf16)
        dh += nt(dqk, wqk) + nt(dvt, wvo)
        left += [dqk, dvt]
        right += [jnp.zeros_like(o), o]
    keep, send = split_halves(core, dh)
    keep_ref[...] = keep
    send_ref[...] = send.astype(send_ref.dtype)
    grad = tn(h, jnp.concatenate(left, axis=1)) + tn(db, jnp.concatenate(right, axis=1))
    acc[...] = grad.astype(acc.dtype)
    scatter_blocks(acc, me, grads)


def mlp_bwd_kernel(parts, rows_at, scal, x_up, own, other, g_ref, rows_ref, extra, x_ref, *refs):
    me, core = scal[0], scal[1]
    refs = list(refs)
    blocks = [refs.pop(0) for _ in range(parts)]
    g_out, small_out, keep_ref, send_ref = [refs.pop(0) for _ in range(4)]
    grads = [refs.pop(0) for _ in range(parts)]
    up, down, acc = refs
    assemble(up, me, blocks, (0,))
    assemble(down, me, blocks, (1,))
    up_row, gain_row = rows_at
    g, small = plain_pull(x_up, own, other, g_ref, rows_ref, extra, up_row, core)
    g_out[...] = g
    small_out[...] = small
    hat, _ = norm_parts(x_ref[...])
    h = (hat * rows_ref[gain_row : gain_row + 1, :]).astype(bf16)
    dm = g.astype(bf16)
    u = nn(h, up[...].astype(bf16))
    cdf = 0.5 * (1.0 + lax.erf(u * root_half))
    r = (u * cdf).astype(bf16)
    slope = cdf + u * inv_root_two_pi * jnp.exp(-0.5 * u * u)
    du = (nn(dm, down[...].astype(bf16)) * slope).astype(bf16)
    keep, send = split_halves(core, nt(du, up[...].astype(bf16)))
    keep_ref[...] = keep
    send_ref[...] = send.astype(send_ref.dtype)
    acc[...] = tn(h, du).astype(acc.dtype)
    scatter_blocks(acc, me, grads, (0,))
    acc[...] = tn(dm, r).astype(acc.dtype)
    scatter_blocks(acc, me, grads, (1,))


def final_kernel(tokens, gain_row, scal, x_ref, own, other, g_ref, rows_ref, extra, g_out, *refs):
    me, core = scal[0], scal[1]
    grads, acc = refs[:-1], refs[-1]
    g, small = plain_pull(x_ref, own, other, g_ref, rows_ref, extra, gain_row, core)
    g_out[...] = g[:tokens]
    eye = (
        lax.broadcasted_iota(jnp.int32, (8, 128), 0) == lax.broadcasted_iota(jnp.int32, (8, 128), 1)
    ).astype(f32)
    acc[...] = lax.dot_general(
        small, eye, (((0,), (0,)), ((), ())), precision=highest, preferred_element_type=f32
    )
    scatter_blocks(acc, me, grads)


def run(kernel, scal, ins, outs, scratch, flops, vmem_mib=24):
    vmem = pl.BlockSpec(memory_space=pltpu.VMEM)
    size = lambda s: s.size * s.dtype.itemsize
    return pl.pallas_call(
        kernel,
        out_shape=outs,
        in_specs=[pl.BlockSpec(memory_space=pltpu.SMEM)] + [vmem] * len(ins),
        out_specs=[vmem] * len(outs),
        scratch_shapes=scratch,
        compiler_params=pltpu.CompilerParams(vmem_limit_bytes=vmem_mib * 2**20),
        cost_estimate=pl.CostEstimate(
            flops=int(flops),
            bytes_accessed=int(sum(size(a) for a in ins) + sum(size(o) for o in outs)),
            transcendentals=0,
        ),
    )(scal, *ins)


def shape(dims, kind):
    return jax.ShapeDtypeStruct(tuple(dims), kind)


def tie(value, *after):
    return lax.optimization_barrier((value,) + after)[0]


def bar(*values):
    return lax.optimization_barrier(values)


def shards(
    fsdp,
    tensor,
    activations,
    image_live,
    expert_routes,
    attn_gain_one,
    qkv_weight_one,
    out_weight_one,
    first_feedforward_gain,
    up_weight_one,
    down_weight_one,
    attn_gain_two,
    qkv_weight_two,
    out_weight_two,
    moe_gain_two,
    router_weight,
    expert_up,
    expert_down,
    cotangent,
):
    parts = fsdp // PLANES
    tokens, model = activations.shape[1:]
    padded = -(-(tokens + 8) // 16) * 16
    half = model // 2
    rows = model // fsdp
    heads = qkv_weight_one.shape[2] // HD
    hidden = up_weight_one.shape[1]
    held = bf16 if rows % 16 == 0 else f32
    me = lax.axis_index("fsdp")
    place = lax.axis_index("tensor")
    core, plane = place % 2, me // parts
    scal = jnp.stack([me, core, plane, place]).astype(jnp.int32)

    def across(value, k):
        return lax.ppermute(value, "fsdp", [(i, i ^ k) for i in range(fsdp)])

    def over(value, k):
        return lax.ppermute(value, "tensor", [(i, i ^ k) for i in range(tensor)])

    def spread(stacked):
        arrays, bit = [stacked], 1
        while bit < parts:
            arrays += [across(a, bit) for a in arrays]
            bit *= 2
        return arrays

    def gather_planes(block):
        return jnp.stack([block] + [across(block, m * parts) for m in range(1, PLANES)])

    def planes(blocks):
        return [blocks[0]] + [across(blocks[m].astype(bf16), m * parts) for m in range(1, PLANES)]

    def added(arrays):
        return sum([a.astype(f32) for a in arrays[1:]], arrays[0].astype(f32))

    def enclosed(stage, *operands):
        def idle(*args):
            return jax.tree.map(lambda r: jnp.zeros(r.shape, r.dtype), jax.eval_shape(stage, *args))

        return lax.cond(me < fsdp, stage, idle, *operands)

    def fold_start(arrays):
        arrays, bit = list(arrays), parts // 2
        while bit > 1:
            for a in range(bit):
                arrays[a] = arrays[a].astype(f32) + across(arrays[a + bit].astype(bf16), bit).astype(f32)
            bit //= 2
        return [arrays[0], across(arrays[1].astype(bf16), 1)] if bit else arrays[:1]

    def fold(arrays):
        arrays, bit = list(arrays), parts // 2
        while bit:
            for a in range(bit):
                arrays[a] = arrays[a].astype(f32) + across(arrays[a + bit].astype(bf16), bit).astype(f32)
            bit //= 2
        return arrays[0]

    def reduce_planes(stacked):
        total = stacked[0].astype(f32)
        for m in range(1, PLANES):
            total = total + across(stacked[m].astype(bf16), m * parts).astype(f32)
        return total

    def pair(total):
        low = total.astype(bf16)
        total = (low.astype(f32) + over(low, 2).astype(f32)).astype(bf16)
        return total, over(total, 1)

    def joined(keep, send):
        return pair(keep + over(send, 1).astype(f32))

    def attn_pack(qkv, out):
        by_head = jnp.moveaxis(qkv.reshape(3, rows, heads, HD), 0, 2)
        out = out.reshape(heads, HD, rows).transpose(2, 0, 1)[:, :, None]
        return jnp.concatenate([by_head, out], axis=2).reshape(rows, heads * 4 * HD)

    def attn_unpack(grad):
        grad = grad.reshape(rows, heads, 4, HD)
        qkv = jnp.moveaxis(grad[:, :, :3], 2, 0).reshape(3, rows, heads * HD)
        return qkv, grad[:, :, 3].transpose(1, 2, 0).reshape(heads * HD, rows)

    smalls = jnp.concatenate(
        [
            router_weight,
            attn_gain_one[:, None],
            first_feedforward_gain[:, None],
            attn_gain_two[:, None],
            moe_gain_two[:, None],
        ],
        axis=1,
    )
    smalls = jnp.pad(smalls, ((0, 0), (0, 128 - smalls.shape[1])))
    one = jnp.concatenate([attn_pack(qkv_weight_one, out_weight_one), smalls], axis=1)
    one = gather_planes(one)
    w_one = spread(one)
    mlp = jnp.stack([up_weight_one, down_weight_one.T])
    mlp = gather_planes(tie(mlp, one))
    w_mlp = spread(mlp)
    two = gather_planes(tie(attn_pack(qkv_weight_two, out_weight_two), mlp))

    def by_plane(experts):
        return [lax.dynamic_index_in_dim(experts, plane ^ m, 0, keepdims=False) for m in range(PLANES)]

    e_up = planes(tie(by_plane(expert_up), two))
    e_down = by_plane(jnp.swapaxes(expert_down, 1, 2))

    pad = ((0, padded - tokens), (0, 0))
    stream0 = jnp.pad(activations[0], pad)
    grad3 = jnp.pad(cotangent[0] * image_live[0].astype(f32), pad)
    routes = jnp.pad(expert_routes[0], pad, constant_values=-1)
    grad_low = grad3.astype(bf16)
    grad_half = jnp.where(core == 0, grad_low[:, :half], grad_low[:, half:])

    stream = shape((padded, model), f32)
    pieces = [shape((padded, half), f32), shape((padded, half), bf16)]
    wide = pltpu.VMEM((model, model + 128), held)
    square = pltpu.VMEM((model, model), held)
    unit = 2 * padded * model * model

    keep, send, small_rows = run(
        functools.partial(attn_fwd_kernel, tokens, parts, 4, True),
        scal,
        [stream0] + w_one,
        pieces + [shape((8, model), f32)],
        [wide],
        3 * unit,
    )
    own, other = joined(keep, send)
    own, other, two, e_up, e_down = bar(own, other, two, e_up, e_down)
    w_two, e_down = spread(two), planes(e_down)

    def stage_two(scal, *ins):
        stream1, keep, send = run(
            functools.partial(mlp_fwd_kernel, parts, 5),
            scal,
            ins,
            [stream] + pieces,
            [square, square],
            2 * unit,
        )
        return stream1, *joined(keep, send)

    stream1, own, other = enclosed(stage_two, scal, stream0, own, other, small_rows, *w_mlp)
    own, other, w_two, e_down, grad_half = bar(own, other, w_two, e_down, grad_half)
    w_e_up = spread(jnp.stack(e_up))
    g_near = planes([grad_half] * PLANES)[1:]

    def stage_three(scal, routes, small_rows, *ins):
        stream2, keep, send = run(
            functools.partial(attn_fwd_kernel, tokens, parts, 6, False),
            scal,
            [*ins[:3], small_rows, *ins[3:]],
            [stream] + pieces,
            [square],
            3 * unit,
        )
        outs = run(
            functools.partial(moe_pre_kernel, tokens, 7),
            scal,
            [stream2, *joined(keep, send), small_rows, routes],
            [stream, shape((padded, model), bf16), shape((padded, half), bf16)],
            [],
            unit / 50,
        )
        return stream2, *outs

    stream2, stream3, h_full, h_half = enclosed(
        stage_three, scal, routes, small_rows, stream1, own, other, *w_two
    )
    h_half, w_e_up, g_near = bar(h_half, w_e_up, g_near)
    h_near = planes([h_half] * PLANES)[1:]
    w_moe = w_e_up + spread(jnp.stack(e_down))
    h_blocks = [h_full] + h_near + [over(n, 1) for n in h_near]
    g_blocks = [grad_low] + g_near + [over(n, 1) for n in g_near]
    images = pltpu.VMEM((PLANES, padded, model), bf16)
    image_hidden = pltpu.VMEM((PLANES, padded, hidden), bf16)
    block_pieces = [shape((PLANES, padded, half), f32), shape((PLANES, padded, half), bf16)]
    y_keep, y_send, d_keep, d_send, *expert_grads = run(
        functools.partial(moe_kernel, parts),
        scal,
        h_blocks + g_blocks + w_moe,
        block_pieces * 2 + [shape((PLANES, rows, hidden), bf16)] * (2 * parts),
        [square, square, images, images, image_hidden, image_hidden, images, square],
        24 * unit,
        40,
    )

    def home(keep, send):
        summed = keep + over(send, 1).astype(f32)
        return planes(list(summed))

    block_grads = [shape((PLANES, rows, model), bf16)] * parts
    own, other = pair(added(home(d_keep, d_send)))
    e_up, e_down = fold(expert_grads[:parts]), fold_start(expert_grads[parts:])
    own, other, e_up = bar(own, other, e_up)
    e_up = planes(list(e_up))
    grad2, small, keep, send, *two_sum = run(
        functools.partial(attn_bwd_kernel, tokens, parts, (7, 6), False),
        scal,
        [stream3, own, other, grad3, small_rows, routes, stream2] + w_two,
        [stream, shape((8, model), f32)] + pieces + block_grads,
        [square, square],
        8 * unit,
    )
    keep, send, e_up, e_down = bar(keep, send, e_up, e_down)
    e_down = planes(list(added(e_down)))
    two_sum = fold(two_sum)
    own, other = joined(keep, send)
    own, other, e_down, two_sum = bar(own, other, e_down, two_sum)
    grad1, small, keep, send, *mlp_sum = run(
        functools.partial(mlp_bwd_kernel, parts, (6, 5)),
        scal,
        [stream2, own, other, grad2, small_rows, small, stream1] + w_mlp,
        [stream, shape((8, model), f32)]
        + pieces
        + [shape((PLANES, 2, rows, hidden), bf16)] * parts,
        [square, square, square],
        5 * unit,
    )
    mlp_sum = fold(mlp_sum)
    two_sum = planes(list(two_sum))
    own, other = joined(keep, send)
    y_keep, y_send = bar(y_keep, y_send, keep)[:2]
    y_own = home(y_keep, y_send)
    own, other, mlp_sum, two_sum, y_own = bar(own, other, mlp_sum, two_sum, y_own)
    mlp_sum = planes(list(mlp_sum))
    y_own, y_other = pair(added(y_own))
    grad0, small, keep, send, *one_sum = run(
        functools.partial(attn_bwd_kernel, tokens, parts, (5, 4), True),
        scal,
        [stream1, own, other, grad1, small_rows, small, stream0] + w_one,
        [stream, shape((8, model), f32)] + pieces + block_grads,
        [wide, square],
        8 * unit,
    )
    one_sum = fold(one_sum)
    own, other = joined(keep, send)
    own, other, one_sum, mlp_sum = bar(own, other, one_sum, mlp_sum)
    one_sum = planes(list(one_sum))
    input_grad, *small_grads = run(
        functools.partial(final_kernel, tokens, 4),
        scal,
        [stream0, own, other, grad0, small_rows, small],
        [shape((tokens, model), f32)] + [shape((PLANES, rows, 128), bf16)] * parts,
        [pltpu.VMEM((model, 128), f32)],
        unit / 50,
    )
    small_sum = reduce_planes(fold(small_grads))
    one_sum, two_sum, mlp_sum = added(one_sum), added(two_sum), added(mlp_sum)

    low = jnp.where(core == 0, y_own, y_other)
    high = jnp.where(core == 0, y_other, y_own)
    result = (stream3 + jnp.concatenate([low, high], axis=1).astype(f32))[:tokens]

    bit0, bit1 = plane % 2 == 1, plane // 2 == 1

    def of_expert(came, x):
        a, b = jnp.where(bit0, came[x ^ 1], came[x]), jnp.where(bit0, came[x ^ 3], came[x ^ 2])
        return jnp.where(bit1, b, a).astype(f32)

    grad_up = jnp.stack([of_expert(e_up, x) for x in range(PLANES)])
    grad_down = jnp.stack([of_expert(e_down, x).T for x in range(PLANES)])
    qkv_one, out_one = attn_unpack(one_sum)
    qkv_two, out_two = attn_unpack(two_sum)
    return (
        result[None],
        input_grad[None],
        small_sum[:, 4],
        qkv_one,
        out_one,
        small_sum[:, 5],
        mlp_sum[0],
        mlp_sum[1].T,
        small_sum[:, 6],
        qkv_two,
        out_two,
        small_sum[:, 7],
        small_sum[:, :PLANES],
        grad_up,
        grad_down,
    )


def solution(mesh):
    return jax.shard_map(
        functools.partial(shards, mesh.shape["fsdp"], mesh.shape["tensor"]),
        mesh=mesh,
        in_specs=(
            P("fsdp", None, None),
            P("fsdp"),
            P("fsdp", None, None),
            P("fsdp"),
            P(None, "fsdp", "tensor"),
            P("tensor", "fsdp"),
            P("fsdp"),
            P("fsdp", "tensor"),
            P("tensor", "fsdp"),
            P("fsdp"),
            P(None, "fsdp", "tensor"),
            P("tensor", "fsdp"),
            P("fsdp"),
            P("fsdp", None),
            P(None, "fsdp", "tensor"),
            P(None, "tensor", "fsdp"),
            P("fsdp", None, None),
        ),
        out_specs=(
            P("fsdp", None, None),
            P("fsdp", None, None),
            P("fsdp"),
            P(None, "fsdp", "tensor"),
            P("tensor", "fsdp"),
            P("fsdp"),
            P("fsdp", "tensor"),
            P("tensor", "fsdp"),
            P("fsdp"),
            P(None, "fsdp", "tensor"),
            P("tensor", "fsdp"),
            P("fsdp"),
            P("fsdp", None),
            P(None, "fsdp", "tensor"),
            P(None, "tensor", "fsdp"),
        ),
        check_vma=False,
    )
```

```python
import functools

import jax
import jax.numpy as jnp
from jax import lax
from jax.experimental import pallas as pl
from jax.experimental.pallas import tpu as pltpu
from jax.sharding import PartitionSpec as P

HD = 64
PLANES = 4
epsilon = 1e-06
root_half = 0.7071067811865476
inv_root_two_pi = 0.3989422804014327
highest = lax.Precision.HIGHEST
bf16 = jnp.bfloat16
f32 = jnp.float32


def nn(a, b):
    return lax.dot_general(a, b, (((1,), (0,)), ((), ())), preferred_element_type=f32)


def nt(a, b):
    return lax.dot_general(a, b, (((1,), (1,)), ((), ())), preferred_element_type=f32)


def tn(a, b):
    return lax.dot_general(a, b, (((0,), (0,)), ((), ())), preferred_element_type=f32)


def norm_parts(x):
    c = x - jnp.mean(x, axis=-1, keepdims=True)
    rs = lax.rsqrt(jnp.mean(c * c, axis=-1, keepdims=True) + epsilon)
    return c * rs, rs


def norm_pull(x, gain, dh):
    hat, rs = norm_parts(x)
    t = dh * gain
    mean_t = jnp.mean(t, axis=-1, keepdims=True)
    mean_th = jnp.mean(t * hat, axis=-1, keepdims=True)
    return rs * (t - mean_t - hat * mean_th), jnp.sum(dh * hat, axis=0, keepdims=True)


def join_halves(core, own, other):
    low = jnp.where(core == 0, own, other)
    high = jnp.where(core == 0, other, own)
    return jnp.concatenate([low, high], axis=1)


def split_halves(core, full):
    half = full.shape[1] // 2
    low, high = full[:, :half], full[:, half:]
    return jnp.where(core == 0, low, high), jnp.where(core == 0, high, low)


def row_of(index, shape):
    return lax.broadcasted_iota(jnp.int32, shape, 0) == index


def assemble(dst, me, refs, pick=()):
    parts = len(refs)
    rows = dst.shape[0] // (parts * PLANES)
    for a, ref in enumerate(refs):
        for m in range(PLANES):
            start = pl.multiple_of((me ^ (m * parts + a)) * rows, rows)
            dst[pl.ds(start, rows), :] = ref[(m,) + pick].astype(dst.dtype)


def scatter_blocks(src, me, refs, pick=()):
    parts = len(refs)
    rows = src.shape[0] // (parts * PLANES)
    for a, ref in enumerate(refs):
        for m in range(PLANES):
            start = pl.multiple_of((me ^ (m * parts + a)) * rows, rows)
            ref[(m,) + pick] = src[pl.ds(start, rows), :].astype(ref.dtype)


def head_tiles(y, head):
    at = 256 * head
    qk, vt = y[:, at : at + 128], y[:, at + 128 : at + 256]
    low = lax.broadcasted_iota(jnp.int32, qk.shape, 1) < HD
    q = jnp.where(low, qk, 0.0).astype(bf16)
    k = jnp.where(low, pltpu.roll(qk, HD, 1), 0.0).astype(bf16)
    v = jnp.where(low, 0.0, pltpu.roll(vt, HD, 1)).astype(bf16)
    return q, k, v


def probs_of(q, k, tokens):
    s = nt(q, k) * (HD**-0.5)
    s = jnp.where(lax.broadcasted_iota(jnp.int32, s.shape, 1) < tokens, s, -1e30)
    e = jnp.exp(s - jnp.max(s, axis=-1, keepdims=True))
    return e / jnp.sum(e, axis=-1, keepdims=True)


def attn_fwd_kernel(tokens, parts, gain_row, first, scal, *refs):
    me, core = scal[0], scal[1]
    refs = list(refs)
    x_ref = refs.pop(0)
    if first:
        x = x_ref[...]
    else:
        own, other, rows_ref = refs.pop(0), refs.pop(0), refs.pop(0)
        x = x_ref[...] + join_halves(core, own[...], other[...])
    blocks = [refs.pop(0) for _ in range(parts)]
    if first:
        keep_ref, send_ref, rows_ref, w = refs
    else:
        x_out, keep_ref, send_ref, w = refs
    assemble(w, me, blocks)
    model = w.shape[0]
    if first:
        eye = (
            lax.broadcasted_iota(jnp.int32, (8, 128), 0)
            == lax.broadcasted_iota(jnp.int32, (8, 128), 1)
        ).astype(bf16)
        rows_ref[...] = nt(eye, w[:, model:].astype(bf16))
    else:
        x_out[...] = x
    hat, _ = norm_parts(x)
    h = (hat * rows_ref[gain_row : gain_row + 1, :]).astype(bf16)
    y = nn(h, w[:, :model].astype(bf16))
    branch = jnp.zeros(x.shape, f32)
    for head in range(model // 256):
        q, k, v = head_tiles(y, head)
        p = probs_of(q, k, tokens).astype(bf16)
        o = nn(p, v).astype(bf16)
        at = 256 * head + 128
        branch += nt(o, w[:, at : at + 128].astype(bf16))
    keep, send = split_halves(core, branch)
    keep_ref[...] = keep
    send_ref[...] = send.astype(send_ref.dtype)


def mlp_fwd_kernel(parts, gain_row, scal, x_ref, own, other, rows_ref, *refs):
    me, core = scal[0], scal[1]
    blocks, (x_out, keep_ref, send_ref, up, down) = refs[:parts], refs[parts:]
    assemble(up, me, blocks, (0,))
    assemble(down, me, blocks, (1,))
    x = x_ref[...] + join_halves(core, own[...], other[...])
    x_out[...] = x
    hat, _ = norm_parts(x)
    h = (hat * rows_ref[gain_row : gain_row + 1, :]).astype(bf16)
    u = nn(h, up[...].astype(bf16))
    r = (0.5 * u * (1.0 + lax.erf(u * root_half))).astype(bf16)
    keep, send = split_halves(core, nt(r, down[...].astype(bf16)))
    keep_ref[...] = keep
    send_ref[...] = send.astype(send_ref.dtype)


def router_probs(h, rows_ref):
    logits = nt(h, rows_ref[...].astype(bf16))
    lane = lax.broadcasted_iota(jnp.int32, logits.shape, 1)
    logits = jnp.where(lane < PLANES, logits, -1e30)
    e = jnp.exp(logits - jnp.max(logits, axis=-1, keepdims=True))
    return e / jnp.sum(e, axis=-1, keepdims=True), lane


def routed(routes, lane):
    return (routes[:, 0:1] == lane) | (routes[:, 1:2] == lane)


def moe_pre_kernel(tokens, gain_row, scal, x_ref, own, other, rows_ref, routes, x_out, h_out, half_out):
    core = scal[1]
    x = x_ref[...] + join_halves(core, own[...], other[...])
    x_out[...] = x
    hat, _ = norm_parts(x)
    h = (hat * rows_ref[gain_row : gain_row + 1, :]).astype(bf16)
    probs, lane = router_probs(h, rows_ref)
    gates = jnp.where(routed(routes[...], lane), probs, 0.0).astype(bf16)
    eye = (
        lax.broadcasted_iota(jnp.int32, (8, 8), 0) == lax.broadcasted_iota(jnp.int32, (8, 8), 1)
    ).astype(bf16)
    gate_rows = nt(eye, gates)
    padded, model = x.shape
    half = model // 2
    live = lax.broadcasted_iota(jnp.int32, x.shape, 0) < tokens
    h = jnp.where(live, h.astype(f32), 0.0)
    wide = jnp.concatenate([gate_rows, jnp.zeros((8, half - padded), f32)], axis=1)
    block = jnp.concatenate([jnp.zeros((padded - 8, half), f32), wide], axis=0)
    low, high = h[:, :half] + block, h[:, half:] + block
    h_out[...] = jnp.concatenate([low, high], axis=1).astype(bf16)
    half_out[...] = jnp.where(core == 0, low, high).astype(bf16)


def moe_kernel(parts, scal, *refs):
    me, core, expert = scal[0], scal[1], scal[2]
    refs = list(refs)
    h_refs = [refs.pop(0) for _ in range(1 + 2 * (PLANES - 1))]
    g_refs = [refs.pop(0) for _ in range(1 + 2 * (PLANES - 1))]
    blocks = [refs.pop(0) for _ in range(2 * parts)]
    y_keep, y_send, d_keep, d_send = [refs.pop(0) for _ in range(4)]
    grads = [refs.pop(0) for _ in range(2 * parts)]
    up, down, hs, gs, rs, dus, dys, acc = refs
    assemble(up, me, blocks[:parts])
    assemble(down, me, blocks[parts:])
    for dst, src in ((hs, h_refs), (gs, g_refs)):
        dst[0] = src[0][...]
        for m in range(1, PLANES):
            dst[m] = join_halves(core, src[m][...], src[PLANES - 1 + m][...])
    padded, model = hs.shape[1:]
    half = model // 2

    def step(m, carry):
        h, g = hs[m], gs[m]
        rows = h.astype(f32)[padded - 8 :, :256]
        pick = row_of(expert, (8, 128)).astype(f32)
        gate = tn(rows, pick)[:padded, :1]
        u = nn(h, up[...].astype(bf16))
        cdf = 0.5 * (1.0 + lax.erf(u * root_half))
        r = (u * cdf).astype(bf16)
        t = nn(g, down[...].astype(bf16))
        slope = cdf + u * inv_root_two_pi * jnp.exp(-0.5 * u * u)
        du = (gate * t * slope).astype(bf16)
        rs[m] = r
        dus[m] = du
        dys[m] = (gate * g.astype(f32)).astype(bf16)
        dots = nt(jnp.ones((8, r.shape[1]), bf16), (r.astype(f32) * t).astype(bf16))
        dots = jnp.where(row_of(expert, dots.shape), dots, 0.0)
        y = gate * nt(r, down[...].astype(bf16))
        keep, send = split_halves(core, y)
        y_keep[m] = keep
        y_send[m] = send.astype(y_send.dtype)
        dh = nt(du, up[...].astype(bf16))
        wide = jnp.concatenate([dots, jnp.zeros((8, model - padded), f32)], axis=1)
        dh = dh + jnp.concatenate([jnp.zeros((padded - 8, model), f32), wide], axis=0)
        keep, send = split_halves(core, dh)
        d_keep[m] = keep
        d_send[m] = send.astype(d_send.dtype)
        return carry

    lax.fori_loop(0, PLANES, step, 0)
    flat = (PLANES * padded, model)
    acc[...] = tn(hs[...].reshape(flat), dus[...].reshape(flat)).astype(acc.dtype)
    scatter_blocks(acc, me, grads[:parts])
    acc[...] = tn(dys[...].reshape(flat), rs[...].reshape(flat)).astype(acc.dtype)
    scatter_blocks(acc, me, grads[parts:])


def plain_pull(x_ref, own, other, g_ref, rows_ref, small_ref, gain_row, core):
    dh = join_halves(core, own[...], other[...]).astype(f32)
    dx, dgain = norm_pull(x_ref[...], rows_ref[gain_row : gain_row + 1, :], dh)
    small = small_ref[...] + jnp.where(row_of(gain_row, small_ref.shape), dgain, 0.0)
    return g_ref[...] + dx, small


def router_pull(tokens, x_ref, own, other, g_ref, rows_ref, routes, gain_row, core):
    dh = join_halves(core, own[...], other[...]).astype(f32)
    padded, model = dh.shape
    gain = rows_ref[gain_row : gain_row + 1, :]
    hat, _ = norm_parts(x_ref[...])
    live = lax.broadcasted_iota(jnp.int32, dh.shape, 0) < tokens
    h = (hat * gain).astype(bf16)
    probs, lane = router_probs(h, rows_ref)
    dots = dh[padded - 8 :, :256]
    eye = (
        lax.broadcasted_iota(jnp.int32, (8, 8), 0) == lax.broadcasted_iota(jnp.int32, (8, 8), 1)
    ).astype(f32)
    dprobs = lax.dot_general(
        dots, eye, (((0,), (0,)), ((), ())), precision=highest, preferred_element_type=f32
    )[:padded]
    keep = routed(routes[...], lane) & (lax.broadcasted_iota(jnp.int32, lane.shape, 0) < tokens)
    dprobs = jnp.where(keep, dprobs, 0.0)
    dlogits = probs * (dprobs - jnp.sum(probs * dprobs, axis=-1, keepdims=True))
    small = lax.dot_general(
        dlogits, h.astype(f32), (((0,), (0,)), ((), ())), precision=highest, preferred_element_type=f32
    )
    router = jnp.where(lax.broadcasted_iota(jnp.int32, small.shape, 0) < PLANES, rows_ref[...], 0.0)
    dh = jnp.where(live, dh, 0.0) + lax.dot_general(
        dlogits, router, (((1,), (0,)), ((), ())), precision=highest, preferred_element_type=f32
    )
    dx, dgain = norm_pull(x_ref[...], gain, dh)
    small = small + jnp.where(row_of(gain_row, small.shape), dgain, 0.0)
    return g_ref[...] + dx, small


def attn_bwd_kernel(tokens, parts, rows_at, last, scal, *refs):
    me, core = scal[0], scal[1]
    refs = list(refs)
    x_up, own, other, g_ref, rows_ref, extra, x_ref = [refs.pop(0) for _ in range(7)]
    blocks = [refs.pop(0) for _ in range(parts)]
    g_out, small_out, keep_ref, send_ref = [refs.pop(0) for _ in range(4)]
    grads = [refs.pop(0) for _ in range(parts)]
    w, acc = refs
    assemble(w, me, blocks)
    up_row, gain_row = rows_at
    if last:
        g, small = plain_pull(x_up, own, other, g_ref, rows_ref, extra, up_row, core)
    else:
        g, small = router_pull(tokens, x_up, own, other, g_ref, rows_ref, extra, up_row, core)
    g_out[...] = g
    small_out[...] = small
    model = acc.shape[1]
    hat, _ = norm_parts(x_ref[...])
    h = (hat * rows_ref[gain_row : gain_row + 1, :]).astype(bf16)
    db = g.astype(bf16)
    y = nn(h, w[:, :model].astype(bf16))
    dh = jnp.zeros(g.shape, f32)
    left, right = [], []
    for head in range(model // 256):
        at = 256 * head
        q, k, v = head_tiles(y, head)
        p = probs_of(q, k, tokens)
        pb = p.astype(bf16)
        o = nn(pb, v).astype(bf16)
        wqk = w[:, at : at + 128].astype(bf16)
        wvo = w[:, at + 128 : at + 256].astype(bf16)
        do = nn(db, wvo)
        low = lax.broadcasted_iota(jnp.int32, do.shape, 1) < HD
        do = jnp.where(low, 0.0, do).astype(bf16)
        dp = nt(do, v)
        dv = tn(pb, do)
        ds = (p * (dp - jnp.sum(p * dp, axis=-1, keepdims=True))).astype(bf16)
        dq = nn(ds, k) * (HD**-0.5)
        dk = tn(ds, q) * (HD**-0.5)
        dqk = (dq + pltpu.roll(dk, HD, 1)).astype(bf16)
        dvt = pltpu.roll(dv, HD, 1).astype(bf16)
        dh += nt(dqk, wqk) + nt(dvt, wvo)
        left += [dqk, dvt]
        right += [jnp.zeros_like(o), o]
    keep, send = split_halves(core, dh)
    keep_ref[...] = keep
    send_ref[...] = send.astype(send_ref.dtype)
    grad = tn(h, jnp.concatenate(left, axis=1)) + tn(db, jnp.concatenate(right, axis=1))
    acc[...] = grad.astype(acc.dtype)
    scatter_blocks(acc, me, grads)


def mlp_bwd_kernel(parts, rows_at, scal, x_up, own, other, g_ref, rows_ref, extra, x_ref, *refs):
    me, core = scal[0], scal[1]
    refs = list(refs)
    blocks = [refs.pop(0) for _ in range(parts)]
    g_out, small_out, keep_ref, send_ref = [refs.pop(0) for _ in range(4)]
    grads = [refs.pop(0) for _ in range(parts)]
    up, down, acc = refs
    assemble(up, me, blocks, (0,))
    assemble(down, me, blocks, (1,))
    up_row, gain_row = rows_at
    g, small = plain_pull(x_up, own, other, g_ref, rows_ref, extra, up_row, core)
    g_out[...] = g
    small_out[...] = small
    hat, _ = norm_parts(x_ref[...])
    h = (hat * rows_ref[gain_row : gain_row + 1, :]).astype(bf16)
    dm = g.astype(bf16)
    u = nn(h, up[...].astype(bf16))
    cdf = 0.5 * (1.0 + lax.erf(u * root_half))
    r = (u * cdf).astype(bf16)
    slope = cdf + u * inv_root_two_pi * jnp.exp(-0.5 * u * u)
    du = (nn(dm, down[...].astype(bf16)) * slope).astype(bf16)
    keep, send = split_halves(core, nt(du, up[...].astype(bf16)))
    keep_ref[...] = keep
    send_ref[...] = send.astype(send_ref.dtype)
    acc[...] = tn(h, du).astype(acc.dtype)
    scatter_blocks(acc, me, grads, (0,))
    acc[...] = tn(dm, r).astype(acc.dtype)
    scatter_blocks(acc, me, grads, (1,))


def final_kernel(tokens, gain_row, scal, x_ref, own, other, g_ref, rows_ref, extra, g_out, *refs):
    me, core = scal[0], scal[1]
    grads, acc = refs[:-1], refs[-1]
    g, small = plain_pull(x_ref, own, other, g_ref, rows_ref, extra, gain_row, core)
    g_out[...] = g[:tokens]
    eye = (
        lax.broadcasted_iota(jnp.int32, (8, 128), 0) == lax.broadcasted_iota(jnp.int32, (8, 128), 1)
    ).astype(f32)
    acc[...] = lax.dot_general(
        small, eye, (((0,), (0,)), ((), ())), precision=highest, preferred_element_type=f32
    )
    scatter_blocks(acc, me, grads)


def run(kernel, scal, ins, outs, scratch, flops, vmem_mib=24):
    vmem = pl.BlockSpec(memory_space=pltpu.VMEM)
    size = lambda s: s.size * s.dtype.itemsize
    return pl.pallas_call(
        kernel,
        out_shape=outs,
        in_specs=[pl.BlockSpec(memory_space=pltpu.SMEM)] + [vmem] * len(ins),
        out_specs=[vmem] * len(outs),
        scratch_shapes=scratch,
        compiler_params=pltpu.CompilerParams(vmem_limit_bytes=vmem_mib * 2**20),
        cost_estimate=pl.CostEstimate(
            flops=int(flops),
            bytes_accessed=int(sum(size(a) for a in ins) + sum(size(o) for o in outs)),
            transcendentals=0,
        ),
    )(scal, *ins)


def shape(dims, kind):
    return jax.ShapeDtypeStruct(tuple(dims), kind)


def tie(value, *after):
    return lax.optimization_barrier((value,) + after)[0]


def bar(*values):
    return lax.optimization_barrier(values)


def shards(
    fsdp,
    tensor,
    activations,
    image_live,
    expert_routes,
    attn_gain_one,
    qkv_weight_one,
    out_weight_one,
    first_feedforward_gain,
    up_weight_one,
    down_weight_one,
    attn_gain_two,
    qkv_weight_two,
    out_weight_two,
    moe_gain_two,
    router_weight,
    expert_up,
    expert_down,
    cotangent,
):
    parts = fsdp // PLANES
    tokens, model = activations.shape[1:]
    padded = -(-(tokens + 8) // 16) * 16
    half = model // 2
    rows = model // fsdp
    heads = qkv_weight_one.shape[2] // HD
    hidden = up_weight_one.shape[1]
    held = bf16 if rows % 16 == 0 else f32
    me = lax.axis_index("fsdp")
    place = lax.axis_index("tensor")
    core, plane = place % 2, me // parts
    scal = jnp.stack([me, core, plane, place]).astype(jnp.int32)

    def across(value, k):
        return lax.ppermute(value, "fsdp", [(i, i ^ k) for i in range(fsdp)])

    def over(value, k):
        return lax.ppermute(value, "tensor", [(i, i ^ k) for i in range(tensor)])

    def spread(stacked):
        arrays, bit = [stacked], 1
        while bit < parts:
            arrays += [across(a, bit) for a in arrays]
            bit *= 2
        return arrays

    def gather_planes(block):
        return jnp.stack([block] + [across(block, m * parts) for m in range(1, PLANES)])

    def planes(blocks):
        return [blocks[0]] + [across(blocks[m].astype(bf16), m * parts) for m in range(1, PLANES)]

    def added(arrays):
        return sum([a.astype(f32) for a in arrays[1:]], arrays[0].astype(f32))

    def enclosed(stage, *operands):
        def idle(*args):
            return jax.tree.map(lambda r: jnp.zeros(r.shape, r.dtype), jax.eval_shape(stage, *args))

        return lax.cond(me < fsdp, stage, idle, *operands)

    def fold_start(arrays):
        arrays, bit = list(arrays), parts // 2
        while bit > 1:
            for a in range(bit):
                arrays[a] = arrays[a].astype(f32) + across(arrays[a + bit].astype(bf16), bit).astype(f32)
            bit //= 2
        return [arrays[0], across(arrays[1].astype(bf16), 1)] if bit else arrays[:1]

    def fold(arrays):
        arrays, bit = list(arrays), parts // 2
        while bit:
            for a in range(bit):
                arrays[a] = arrays[a].astype(f32) + across(arrays[a + bit].astype(bf16), bit).astype(f32)
            bit //= 2
        return arrays[0]

    def reduce_planes(stacked):
        total = stacked[0].astype(f32)
        for m in range(1, PLANES):
            total = total + across(stacked[m].astype(bf16), m * parts).astype(f32)
        return total

    def pair(total):
        low = total.astype(bf16)
        total = (low.astype(f32) + over(low, 2).astype(f32)).astype(bf16)
        return total, over(total, 1)

    def joined(keep, send):
        return pair(keep + over(send, 1).astype(f32))

    def attn_pack(qkv, out):
        by_head = jnp.moveaxis(qkv.reshape(3, rows, heads, HD), 0, 2)
        out = out.reshape(heads, HD, rows).transpose(2, 0, 1)[:, :, None]
        return jnp.concatenate([by_head, out], axis=2).reshape(rows, heads * 4 * HD)

    def attn_unpack(grad):
        grad = grad.reshape(rows, heads, 4, HD)
        qkv = jnp.moveaxis(grad[:, :, :3], 2, 0).reshape(3, rows, heads * HD)
        return qkv, grad[:, :, 3].transpose(1, 2, 0).reshape(heads * HD, rows)

    smalls = jnp.concatenate(
        [
            router_weight,
            attn_gain_one[:, None],
            first_feedforward_gain[:, None],
            attn_gain_two[:, None],
            moe_gain_two[:, None],
        ],
        axis=1,
    )
    smalls = jnp.pad(smalls, ((0, 0), (0, 128 - smalls.shape[1])))
    one = jnp.concatenate([attn_pack(qkv_weight_one, out_weight_one), smalls], axis=1)
    one = gather_planes(one)
    w_one = spread(one)
    mlp = jnp.stack([up_weight_one, down_weight_one.T])
    mlp = gather_planes(tie(mlp, one))
    w_mlp = spread(mlp)
    two = gather_planes(tie(attn_pack(qkv_weight_two, out_weight_two), mlp))

    def by_plane(experts):
        return [lax.dynamic_index_in_dim(experts, plane ^ m, 0, keepdims=False) for m in range(PLANES)]

    e_up = planes(tie(by_plane(expert_up), two))
    e_down = by_plane(jnp.swapaxes(expert_down, 1, 2))

    pad = ((0, padded - tokens), (0, 0))
    stream0 = jnp.pad(activations[0], pad)
    grad3 = jnp.pad(cotangent[0] * image_live[0].astype(f32), pad)
    routes = jnp.pad(expert_routes[0], pad, constant_values=-1)
    grad_low = grad3.astype(bf16)
    grad_half = jnp.where(core == 0, grad_low[:, :half], grad_low[:, half:])

    stream = shape((padded, model), f32)
    pieces = [shape((padded, half), f32), shape((padded, half), bf16)]
    wide = pltpu.VMEM((model, model + 128), held)
    square = pltpu.VMEM((model, model), held)
    unit = 2 * padded * model * model

    keep, send, small_rows = run(
        functools.partial(attn_fwd_kernel, tokens, parts, 4, True),
        scal,
        [stream0] + w_one,
        pieces + [shape((8, model), f32)],
        [wide],
        3 * unit,
    )
    own, other = joined(keep, send)
    own, other, two, e_up, e_down = bar(own, other, two, e_up, e_down)
    w_two, e_down = spread(two), planes(e_down)

    def stage_two(scal, *ins):
        stream1, keep, send = run(
            functools.partial(mlp_fwd_kernel, parts, 5),
            scal,
            ins,
            [stream] + pieces,
            [square, square],
            2 * unit,
        )
        return stream1, *joined(keep, send)

    stream1, own, other = enclosed(stage_two, scal, stream0, own, other, small_rows, *w_mlp)
    own, other, w_two, e_down, grad_half = bar(own, other, w_two, e_down, grad_half)
    w_e_up = spread(jnp.stack(e_up))
    g_near = planes([grad_half] * PLANES)[1:]

    def stage_three(scal, routes, small_rows, *ins):
        stream2, keep, send = run(
            functools.partial(attn_fwd_kernel, tokens, parts, 6, False),
            scal,
            [*ins[:3], small_rows, *ins[3:]],
            [stream] + pieces,
            [square],
            3 * unit,
        )
        outs = run(
            functools.partial(moe_pre_kernel, tokens, 7),
            scal,
            [stream2, *joined(keep, send), small_rows, routes],
            [stream, shape((padded, model), bf16), shape((padded, half), bf16)],
            [],
            unit / 50,
        )
        return stream2, *outs

    stream2, stream3, h_full, h_half = enclosed(
        stage_three, scal, routes, small_rows, stream1, own, other, *w_two
    )
    h_half, w_e_up, g_near = bar(h_half, w_e_up, g_near)
    h_near = planes([h_half] * PLANES)[1:]
    w_moe = w_e_up + spread(jnp.stack(e_down))
    h_blocks = [h_full] + h_near + [over(n, 1) for n in h_near]
    g_blocks = [grad_low] + g_near + [over(n, 1) for n in g_near]
    images = pltpu.VMEM((PLANES, padded, model), bf16)
    image_hidden = pltpu.VMEM((PLANES, padded, hidden), bf16)
    block_pieces = [shape((PLANES, padded, half), f32), shape((PLANES, padded, half), bf16)]
    y_keep, y_send, d_keep, d_send, *expert_grads = run(
        functools.partial(moe_kernel, parts),
        scal,
        h_blocks + g_blocks + w_moe,
        block_pieces * 2 + [shape((PLANES, rows, hidden), bf16)] * (2 * parts),
        [square, square, images, images, image_hidden, image_hidden, images, square],
        24 * unit,
        40,
    )

    def home(keep, send):
        summed = keep + over(send, 1).astype(f32)
        return planes(list(summed))

    block_grads = [shape((PLANES, rows, model), bf16)] * parts
    own, other = pair(added(home(d_keep, d_send)))
    e_up, e_down = fold(expert_grads[:parts]), fold_start(expert_grads[parts:])
    own, other, e_up = bar(own, other, e_up)
    e_up = planes(list(e_up))
    grad2, small, keep, send, *two_sum = run(
        functools.partial(attn_bwd_kernel, tokens, parts, (7, 6), False),
        scal,
        [stream3, own, other, grad3, small_rows, routes, stream2] + w_two,
        [stream, shape((8, model), f32)] + pieces + block_grads,
        [square, square],
        8 * unit,
    )
    keep, send, e_up, e_down = bar(keep, send, e_up, e_down)
    e_down = planes(list(added(e_down)))
    two_sum = fold(two_sum)
    own, other = joined(keep, send)
    own, other, e_down, two_sum = bar(own, other, e_down, two_sum)
    grad1, small, keep, send, *mlp_sum = run(
        functools.partial(mlp_bwd_kernel, parts, (6, 5)),
        scal,
        [stream2, own, other, grad2, small_rows, small, stream1] + w_mlp,
        [stream, shape((8, model), f32)]
        + pieces
        + [shape((PLANES, 2, rows, hidden), bf16)] * parts,
        [square, square, square],
        5 * unit,
    )
    mlp_sum = fold(mlp_sum)
    two_sum = planes(list(two_sum))
    own, other = joined(keep, send)
    y_keep, y_send = bar(y_keep, y_send, keep)[:2]
    y_own = home(y_keep, y_send)
    own, other, mlp_sum, two_sum, y_own = bar(own, other, mlp_sum, two_sum, y_own)
    mlp_sum = planes(list(mlp_sum))
    y_own, y_other = pair(added(y_own))
    grad0, small, keep, send, *one_sum = run(
        functools.partial(attn_bwd_kernel, tokens, parts, (5, 4), True),
        scal,
        [stream1, own, other, grad1, small_rows, small, stream0] + w_one,
        [stream, shape((8, model), f32)] + pieces + block_grads,
        [wide, square],
        8 * unit,
    )
    keep, send, mlp_sum[1] = bar(keep, send, mlp_sum[1])
    one_sum = fold(one_sum)
    own, other = joined(keep, send)
    own, other, one_sum, mlp_sum = bar(own, other, one_sum, mlp_sum)
    one_sum = planes(list(one_sum))
    input_grad, *small_grads = run(
        functools.partial(final_kernel, tokens, 4),
        scal,
        [stream0, own, other, grad0, small_rows, small],
        [shape((tokens, model), f32)] + [shape((PLANES, rows, 128), bf16)] * parts,
        [pltpu.VMEM((model, 128), f32)],
        unit / 50,
    )
    small_sum = reduce_planes(fold(small_grads))
    one_sum, two_sum, mlp_sum = added(one_sum), added(two_sum), added(mlp_sum)

    low = jnp.where(core == 0, y_own, y_other)
    high = jnp.where(core == 0, y_other, y_own)
    result = (stream3 + jnp.concatenate([low, high], axis=1).astype(f32))[:tokens]

    bit0, bit1 = plane % 2 == 1, plane // 2 == 1

    def of_expert(came, x):
        a, b = jnp.where(bit0, came[x ^ 1], came[x]), jnp.where(bit0, came[x ^ 3], came[x ^ 2])
        return jnp.where(bit1, b, a).astype(f32)

    grad_up = jnp.stack([of_expert(e_up, x) for x in range(PLANES)])
    grad_down = jnp.stack([of_expert(e_down, x).T for x in range(PLANES)])
    qkv_one, out_one = attn_unpack(one_sum)
    qkv_two, out_two = attn_unpack(two_sum)
    return (
        result[None],
        input_grad[None],
        small_sum[:, 4],
        qkv_one,
        out_one,
        small_sum[:, 5],
        mlp_sum[0],
        mlp_sum[1].T,
        small_sum[:, 6],
        qkv_two,
        out_two,
        small_sum[:, 7],
        small_sum[:, :PLANES],
        grad_up,
        grad_down,
    )


def solution(mesh):
    return jax.shard_map(
        functools.partial(shards, mesh.shape["fsdp"], mesh.shape["tensor"]),
        mesh=mesh,
        in_specs=(
            P("fsdp", None, None),
            P("fsdp"),
            P("fsdp", None, None),
            P("fsdp"),
            P(None, "fsdp", "tensor"),
            P("tensor", "fsdp"),
            P("fsdp"),
            P("fsdp", "tensor"),
            P("tensor", "fsdp"),
            P("fsdp"),
            P(None, "fsdp", "tensor"),
            P("tensor", "fsdp"),
            P("fsdp"),
            P("fsdp", None),
            P(None, "fsdp", "tensor"),
            P(None, "tensor", "fsdp"),
            P("fsdp", None, None),
        ),
        out_specs=(
            P("fsdp", None, None),
            P("fsdp", None, None),
            P("fsdp"),
            P(None, "fsdp", "tensor"),
            P("tensor", "fsdp"),
            P("fsdp"),
            P("fsdp", "tensor"),
            P("tensor", "fsdp"),
            P("fsdp"),
            P(None, "fsdp", "tensor"),
            P("tensor", "fsdp"),
            P("fsdp"),
            P("fsdp", None),
            P(None, "fsdp", "tensor"),
            P(None, "tensor", "fsdp"),
        ),
        check_vma=False,
    )
```

```python
import functools

import jax
import jax.numpy as jnp
from jax import lax
from jax.experimental import pallas as pl
from jax.experimental.pallas import tpu as pltpu
from jax.sharding import PartitionSpec as P

HD = 64
PLANES = 4
epsilon = 1e-06
root_half = 0.7071067811865476
inv_root_two_pi = 0.3989422804014327
highest = lax.Precision.HIGHEST
bf16 = jnp.bfloat16
f32 = jnp.float32


def nn(a, b):
    return lax.dot_general(a, b, (((1,), (0,)), ((), ())), preferred_element_type=f32)


def nt(a, b):
    return lax.dot_general(a, b, (((1,), (1,)), ((), ())), preferred_element_type=f32)


def tn(a, b):
    return lax.dot_general(a, b, (((0,), (0,)), ((), ())), preferred_element_type=f32)


def norm_parts(x):
    c = x - jnp.mean(x, axis=-1, keepdims=True)
    rs = lax.rsqrt(jnp.mean(c * c, axis=-1, keepdims=True) + epsilon)
    return c * rs, rs


def norm_pull(x, gain, dh):
    hat, rs = norm_parts(x)
    t = dh * gain
    mean_t = jnp.mean(t, axis=-1, keepdims=True)
    mean_th = jnp.mean(t * hat, axis=-1, keepdims=True)
    return rs * (t - mean_t - hat * mean_th), jnp.sum(dh * hat, axis=0, keepdims=True)


def join_halves(core, own, other):
    low = jnp.where(core == 0, own, other)
    high = jnp.where(core == 0, other, own)
    return jnp.concatenate([low, high], axis=1)


def split_halves(core, full):
    half = full.shape[1] // 2
    low, high = full[:, :half], full[:, half:]
    return jnp.where(core == 0, low, high), jnp.where(core == 0, high, low)


def row_of(index, shape):
    return lax.broadcasted_iota(jnp.int32, shape, 0) == index


def assemble(dst, me, refs, pick=()):
    parts = len(refs)
    rows = dst.shape[0] // (parts * PLANES)
    for a, ref in enumerate(refs):
        for m in range(PLANES):
            start = pl.multiple_of((me ^ (m * parts + a)) * rows, rows)
            dst[pl.ds(start, rows), :] = ref[(m,) + pick].astype(dst.dtype)


def scatter_blocks(src, me, refs, pick=()):
    parts = len(refs)
    rows = src.shape[0] // (parts * PLANES)
    for a, ref in enumerate(refs):
        for m in range(PLANES):
            start = pl.multiple_of((me ^ (m * parts + a)) * rows, rows)
            ref[(m,) + pick] = src[pl.ds(start, rows), :].astype(ref.dtype)


def head_tiles(y, head):
    at = 256 * head
    qk, vt = y[:, at : at + 128], y[:, at + 128 : at + 256]
    low = lax.broadcasted_iota(jnp.int32, qk.shape, 1) < HD
    q = jnp.where(low, qk, 0.0).astype(bf16)
    k = jnp.where(low, pltpu.roll(qk, HD, 1), 0.0).astype(bf16)
    v = jnp.where(low, 0.0, pltpu.roll(vt, HD, 1)).astype(bf16)
    return q, k, v


def probs_of(q, k, tokens):
    s = nt(q, k) * (HD**-0.5)
    s = jnp.where(lax.broadcasted_iota(jnp.int32, s.shape, 1) < tokens, s, -1e30)
    e = jnp.exp(s - jnp.max(s, axis=-1, keepdims=True))
    return e / jnp.sum(e, axis=-1, keepdims=True)


def attn_fwd_kernel(tokens, parts, gain_row, first, scal, *refs):
    me, core = scal[0], scal[1]
    refs = list(refs)
    x_ref = refs.pop(0)
    if first:
        x = x_ref[...]
    else:
        own, other, rows_ref = refs.pop(0), refs.pop(0), refs.pop(0)
        x = x_ref[...] + join_halves(core, own[...], other[...])
    blocks = [refs.pop(0) for _ in range(parts)]
    if first:
        keep_ref, send_ref, rows_ref, w = refs
    else:
        x_out, keep_ref, send_ref, w = refs
    assemble(w, me, blocks)
    model = w.shape[0]
    if first:
        eye = (
            lax.broadcasted_iota(jnp.int32, (8, 128), 0)
            == lax.broadcasted_iota(jnp.int32, (8, 128), 1)
        ).astype(bf16)
        rows_ref[...] = nt(eye, w[:, model:].astype(bf16))
    else:
        x_out[...] = x
    hat, _ = norm_parts(x)
    h = (hat * rows_ref[gain_row : gain_row + 1, :]).astype(bf16)
    y = nn(h, w[:, :model].astype(bf16))
    branch = jnp.zeros(x.shape, f32)
    for head in range(model // 256):
        q, k, v = head_tiles(y, head)
        p = probs_of(q, k, tokens).astype(bf16)
        o = nn(p, v).astype(bf16)
        at = 256 * head + 128
        branch += nt(o, w[:, at : at + 128].astype(bf16))
    keep, send = split_halves(core, branch)
    keep_ref[...] = keep
    send_ref[...] = send.astype(send_ref.dtype)


def mlp_fwd_kernel(parts, gain_row, scal, x_ref, own, other, rows_ref, *refs):
    me, core = scal[0], scal[1]
    blocks, (x_out, keep_ref, send_ref, up, down) = refs[:parts], refs[parts:]
    assemble(up, me, blocks, (0,))
    assemble(down, me, blocks, (1,))
    x = x_ref[...] + join_halves(core, own[...], other[...])
    x_out[...] = x
    hat, _ = norm_parts(x)
    h = (hat * rows_ref[gain_row : gain_row + 1, :]).astype(bf16)
    u = nn(h, up[...].astype(bf16))
    r = (0.5 * u * (1.0 + lax.erf(u * root_half))).astype(bf16)
    keep, send = split_halves(core, nt(r, down[...].astype(bf16)))
    keep_ref[...] = keep
    send_ref[...] = send.astype(send_ref.dtype)


def router_probs(h, rows_ref):
    logits = nt(h, rows_ref[...].astype(bf16))
    lane = lax.broadcasted_iota(jnp.int32, logits.shape, 1)
    logits = jnp.where(lane < PLANES, logits, -1e30)
    e = jnp.exp(logits - jnp.max(logits, axis=-1, keepdims=True))
    return e / jnp.sum(e, axis=-1, keepdims=True), lane


def routed(routes, lane):
    return (routes[:, 0:1] == lane) | (routes[:, 1:2] == lane)


def moe_pre_kernel(tokens, gain_row, scal, x_ref, own, other, rows_ref, routes, x_out, h_out, half_out):
    core = scal[1]
    x = x_ref[...] + join_halves(core, own[...], other[...])
    x_out[...] = x
    hat, _ = norm_parts(x)
    h = (hat * rows_ref[gain_row : gain_row + 1, :]).astype(bf16)
    probs, lane = router_probs(h, rows_ref)
    gates = jnp.where(routed(routes[...], lane), probs, 0.0).astype(bf16)
    eye = (
        lax.broadcasted_iota(jnp.int32, (8, 8), 0) == lax.broadcasted_iota(jnp.int32, (8, 8), 1)
    ).astype(bf16)
    gate_rows = nt(eye, gates)
    padded, model = x.shape
    half = model // 2
    live = lax.broadcasted_iota(jnp.int32, x.shape, 0) < tokens
    h = jnp.where(live, h.astype(f32), 0.0)
    wide = jnp.concatenate([gate_rows, jnp.zeros((8, half - padded), f32)], axis=1)
    block = jnp.concatenate([jnp.zeros((padded - 8, half), f32), wide], axis=0)
    low, high = h[:, :half] + block, h[:, half:] + block
    h_out[...] = jnp.concatenate([low, high], axis=1).astype(bf16)
    half_out[...] = jnp.where(core == 0, low, high).astype(bf16)


def moe_kernel(parts, scal, *refs):
    me, core, expert = scal[0], scal[1], scal[2]
    refs = list(refs)
    h_refs = [refs.pop(0) for _ in range(1 + 2 * (PLANES - 1))]
    g_refs = [refs.pop(0) for _ in range(1 + 2 * (PLANES - 1))]
    blocks = [refs.pop(0) for _ in range(2 * parts)]
    y_keep, y_send, d_keep, d_send = [refs.pop(0) for _ in range(4)]
    grads = [refs.pop(0) for _ in range(2 * parts)]
    up, down, hs, gs, rs, dus, dys, acc = refs
    assemble(up, me, blocks[:parts])
    assemble(down, me, blocks[parts:])
    for dst, src in ((hs, h_refs), (gs, g_refs)):
        dst[0] = src[0][...]
        for m in range(1, PLANES):
            dst[m] = join_halves(core, src[m][...], src[PLANES - 1 + m][...])
    padded, model = hs.shape[1:]
    half = model // 2

    def step(m, carry):
        h, g = hs[m], gs[m]
        rows = h.astype(f32)[padded - 8 :, :256]
        pick = row_of(expert, (8, 128)).astype(f32)
        gate = tn(rows, pick)[:padded, :1]
        u = nn(h, up[...].astype(bf16))
        cdf = 0.5 * (1.0 + lax.erf(u * root_half))
        r = (u * cdf).astype(bf16)
        t = nn(g, down[...].astype(bf16))
        slope = cdf + u * inv_root_two_pi * jnp.exp(-0.5 * u * u)
        du = (gate * t * slope).astype(bf16)
        rs[m] = r
        dus[m] = du
        dys[m] = (gate * g.astype(f32)).astype(bf16)
        dots = nt(jnp.ones((8, r.shape[1]), bf16), (r.astype(f32) * t).astype(bf16))
        dots = jnp.where(row_of(expert, dots.shape), dots, 0.0)
        y = gate * nt(r, down[...].astype(bf16))
        keep, send = split_halves(core, y)
        y_keep[m] = keep
        y_send[m] = send.astype(y_send.dtype)
        dh = nt(du, up[...].astype(bf16))
        wide = jnp.concatenate([dots, jnp.zeros((8, model - padded), f32)], axis=1)
        dh = dh + jnp.concatenate([jnp.zeros((padded - 8, model), f32), wide], axis=0)
        keep, send = split_halves(core, dh)
        d_keep[m] = keep
        d_send[m] = send.astype(d_send.dtype)
        return carry

    lax.fori_loop(0, PLANES, step, 0)
    flat = (PLANES * padded, model)
    acc[...] = tn(hs[...].reshape(flat), dus[...].reshape(flat)).astype(acc.dtype)
    scatter_blocks(acc, me, grads[:parts])
    acc[...] = tn(dys[...].reshape(flat), rs[...].reshape(flat)).astype(acc.dtype)
    scatter_blocks(acc, me, grads[parts:])


def plain_pull(x_ref, own, other, g_ref, rows_ref, small_ref, gain_row, core):
    dh = join_halves(core, own[...], other[...]).astype(f32)
    dx, dgain = norm_pull(x_ref[...], rows_ref[gain_row : gain_row + 1, :], dh)
    small = small_ref[...] + jnp.where(row_of(gain_row, small_ref.shape), dgain, 0.0)
    return g_ref[...] + dx, small


def router_pull(tokens, x_ref, own, other, g_ref, rows_ref, routes, gain_row, core):
    dh = join_halves(core, own[...], other[...]).astype(f32)
    padded, model = dh.shape
    gain = rows_ref[gain_row : gain_row + 1, :]
    hat, _ = norm_parts(x_ref[...])
    live = lax.broadcasted_iota(jnp.int32, dh.shape, 0) < tokens
    h = (hat * gain).astype(bf16)
    probs, lane = router_probs(h, rows_ref)
    dots = dh[padded - 8 :, :256]
    eye = (
        lax.broadcasted_iota(jnp.int32, (8, 8), 0) == lax.broadcasted_iota(jnp.int32, (8, 8), 1)
    ).astype(f32)
    dprobs = lax.dot_general(
        dots, eye, (((0,), (0,)), ((), ())), precision=highest, preferred_element_type=f32
    )[:padded]
    keep = routed(routes[...], lane) & (lax.broadcasted_iota(jnp.int32, lane.shape, 0) < tokens)
    dprobs = jnp.where(keep, dprobs, 0.0)
    dlogits = probs * (dprobs - jnp.sum(probs * dprobs, axis=-1, keepdims=True))
    small = lax.dot_general(
        dlogits, h.astype(f32), (((0,), (0,)), ((), ())), precision=highest, preferred_element_type=f32
    )
    router = jnp.where(lax.broadcasted_iota(jnp.int32, small.shape, 0) < PLANES, rows_ref[...], 0.0)
    dh = jnp.where(live, dh, 0.0) + lax.dot_general(
        dlogits, router, (((1,), (0,)), ((), ())), precision=highest, preferred_element_type=f32
    )
    dx, dgain = norm_pull(x_ref[...], gain, dh)
    small = small + jnp.where(row_of(gain_row, small.shape), dgain, 0.0)
    return g_ref[...] + dx, small


def attn_bwd_kernel(tokens, parts, rows_at, last, scal, *refs):
    me, core = scal[0], scal[1]
    refs = list(refs)
    x_up, own, other, g_ref, rows_ref, extra, x_ref = [refs.pop(0) for _ in range(7)]
    blocks = [refs.pop(0) for _ in range(parts)]
    g_out, small_out, keep_ref, send_ref = [refs.pop(0) for _ in range(4)]
    grads = [refs.pop(0) for _ in range(parts)]
    w, acc = refs
    assemble(w, me, blocks)
    up_row, gain_row = rows_at
    if last:
        g, small = plain_pull(x_up, own, other, g_ref, rows_ref, extra, up_row, core)
    else:
        g, small = router_pull(tokens, x_up, own, other, g_ref, rows_ref, extra, up_row, core)
    g_out[...] = g
    small_out[...] = small
    model = acc.shape[1]
    hat, _ = norm_parts(x_ref[...])
    h = (hat * rows_ref[gain_row : gain_row + 1, :]).astype(bf16)
    db = g.astype(bf16)
    y = nn(h, w[:, :model].astype(bf16))
    dh = jnp.zeros(g.shape, f32)
    left, right = [], []
    for head in range(model // 256):
        at = 256 * head
        q, k, v = head_tiles(y, head)
        p = probs_of(q, k, tokens)
        pb = p.astype(bf16)
        o = nn(pb, v).astype(bf16)
        wqk = w[:, at : at + 128].astype(bf16)
        wvo = w[:, at + 128 : at + 256].astype(bf16)
        do = nn(db, wvo)
        low = lax.broadcasted_iota(jnp.int32, do.shape, 1) < HD
        do = jnp.where(low, 0.0, do).astype(bf16)
        dp = nt(do, v)
        dv = tn(pb, do)
        ds = (p * (dp - jnp.sum(p * dp, axis=-1, keepdims=True))).astype(bf16)
        dq = nn(ds, k) * (HD**-0.5)
        dk = tn(ds, q) * (HD**-0.5)
        dqk = (dq + pltpu.roll(dk, HD, 1)).astype(bf16)
        dvt = pltpu.roll(dv, HD, 1).astype(bf16)
        dh += nt(dqk, wqk) + nt(dvt, wvo)
        left += [dqk, dvt]
        right += [jnp.zeros_like(o), o]
    keep, send = split_halves(core, dh)
    keep_ref[...] = keep
    send_ref[...] = send.astype(send_ref.dtype)
    grad = tn(h, jnp.concatenate(left, axis=1)) + tn(db, jnp.concatenate(right, axis=1))
    acc[...] = grad.astype(acc.dtype)
    scatter_blocks(acc, me, grads)


def mlp_bwd_kernel(parts, rows_at, scal, x_up, own, other, g_ref, rows_ref, extra, x_ref, *refs):
    me, core = scal[0], scal[1]
    refs = list(refs)
    blocks = [refs.pop(0) for _ in range(parts)]
    g_out, small_out, keep_ref, send_ref = [refs.pop(0) for _ in range(4)]
    grads = [refs.pop(0) for _ in range(parts)]
    up, down, acc = refs
    assemble(up, me, blocks, (0,))
    assemble(down, me, blocks, (1,))
    up_row, gain_row = rows_at
    g, small = plain_pull(x_up, own, other, g_ref, rows_ref, extra, up_row, core)
    g_out[...] = g
    small_out[...] = small
    hat, _ = norm_parts(x_ref[...])
    h = (hat * rows_ref[gain_row : gain_row + 1, :]).astype(bf16)
    dm = g.astype(bf16)
    u = nn(h, up[...].astype(bf16))
    cdf = 0.5 * (1.0 + lax.erf(u * root_half))
    r = (u * cdf).astype(bf16)
    slope = cdf + u * inv_root_two_pi * jnp.exp(-0.5 * u * u)
    du = (nn(dm, down[...].astype(bf16)) * slope).astype(bf16)
    keep, send = split_halves(core, nt(du, up[...].astype(bf16)))
    keep_ref[...] = keep
    send_ref[...] = send.astype(send_ref.dtype)
    acc[...] = tn(h, du).astype(acc.dtype)
    scatter_blocks(acc, me, grads, (0,))
    acc[...] = tn(dm, r).astype(acc.dtype)
    scatter_blocks(acc, me, grads, (1,))


def final_kernel(tokens, gain_row, scal, x_ref, own, other, g_ref, rows_ref, extra, g_out, *refs):
    me, core = scal[0], scal[1]
    grads, acc = refs[:-1], refs[-1]
    g, small = plain_pull(x_ref, own, other, g_ref, rows_ref, extra, gain_row, core)
    g_out[...] = g[:tokens]
    eye = (
        lax.broadcasted_iota(jnp.int32, (8, 128), 0) == lax.broadcasted_iota(jnp.int32, (8, 128), 1)
    ).astype(f32)
    acc[...] = lax.dot_general(
        small, eye, (((0,), (0,)), ((), ())), precision=highest, preferred_element_type=f32
    )
    scatter_blocks(acc, me, grads)


def run(kernel, scal, ins, outs, scratch, flops, vmem_mib=24):
    vmem = pl.BlockSpec(memory_space=pltpu.VMEM)
    size = lambda s: s.size * s.dtype.itemsize
    return pl.pallas_call(
        kernel,
        out_shape=outs,
        in_specs=[pl.BlockSpec(memory_space=pltpu.SMEM)] + [vmem] * len(ins),
        out_specs=[vmem] * len(outs),
        scratch_shapes=scratch,
        compiler_params=pltpu.CompilerParams(vmem_limit_bytes=vmem_mib * 2**20),
        cost_estimate=pl.CostEstimate(
            flops=int(flops),
            bytes_accessed=int(sum(size(a) for a in ins) + sum(size(o) for o in outs)),
            transcendentals=0,
        ),
    )(scal, *ins)


def shape(dims, kind):
    return jax.ShapeDtypeStruct(tuple(dims), kind)


def tie(value, *after):
    return lax.optimization_barrier((value,) + after)[0]


def bar(*values):
    return lax.optimization_barrier(values)


def shards(
    fsdp,
    tensor,
    activations,
    image_live,
    expert_routes,
    attn_gain_one,
    qkv_weight_one,
    out_weight_one,
    first_feedforward_gain,
    up_weight_one,
    down_weight_one,
    attn_gain_two,
    qkv_weight_two,
    out_weight_two,
    moe_gain_two,
    router_weight,
    expert_up,
    expert_down,
    cotangent,
):
    parts = fsdp // PLANES
    tokens, model = activations.shape[1:]
    padded = -(-(tokens + 8) // 16) * 16
    half = model // 2
    rows = model // fsdp
    heads = qkv_weight_one.shape[2] // HD
    hidden = up_weight_one.shape[1]
    held = bf16 if rows % 16 == 0 else f32
    me = lax.axis_index("fsdp")
    place = lax.axis_index("tensor")
    core, plane = place % 2, me // parts
    scal = jnp.stack([me, core, plane, place]).astype(jnp.int32)

    def across(value, k):
        return lax.ppermute(value, "fsdp", [(i, i ^ k) for i in range(fsdp)])

    def over(value, k):
        return lax.ppermute(value, "tensor", [(i, i ^ k) for i in range(tensor)])

    def spread(stacked):
        arrays, bit = [stacked], 1
        while bit < parts:
            arrays += [across(a, bit) for a in arrays]
            bit *= 2
        return arrays

    def gather_planes(block):
        return jnp.stack([block] + [across(block, m * parts) for m in range(1, PLANES)])

    def planes(blocks):
        return [blocks[0]] + [across(blocks[m].astype(bf16), m * parts) for m in range(1, PLANES)]

    def added(arrays):
        return sum([a.astype(f32) for a in arrays[1:]], arrays[0].astype(f32))

    def enclosed(stage, *operands):
        def idle(*args):
            return jax.tree.map(lambda r: jnp.zeros(r.shape, r.dtype), jax.eval_shape(stage, *args))

        return lax.cond(me < fsdp, stage, idle, *operands)

    def fold_start(arrays):
        arrays, bit = list(arrays), parts // 2
        while bit > 1:
            for a in range(bit):
                arrays[a] = arrays[a].astype(f32) + across(arrays[a + bit].astype(bf16), bit).astype(f32)
            bit //= 2
        return [arrays[0], across(arrays[1].astype(bf16), 1)] if bit else arrays[:1]

    def fold(arrays):
        arrays, bit = list(arrays), parts // 2
        while bit:
            for a in range(bit):
                arrays[a] = arrays[a].astype(f32) + across(arrays[a + bit].astype(bf16), bit).astype(f32)
            bit //= 2
        return arrays[0]

    def reduce_planes(stacked):
        total = stacked[0].astype(f32)
        for m in range(1, PLANES):
            total = total + across(stacked[m].astype(bf16), m * parts).astype(f32)
        return total

    def pair(total):
        low = total.astype(bf16)
        total = (low.astype(f32) + over(low, 2).astype(f32)).astype(bf16)
        return total, over(total, 1)

    def joined(keep, send):
        return pair(keep + over(send, 1).astype(f32))

    def attn_pack(qkv, out):
        by_head = jnp.moveaxis(qkv.reshape(3, rows, heads, HD), 0, 2)
        out = out.reshape(heads, HD, rows).transpose(2, 0, 1)[:, :, None]
        return jnp.concatenate([by_head, out], axis=2).reshape(rows, heads * 4 * HD)

    def attn_unpack(grad):
        grad = grad.reshape(rows, heads, 4, HD)
        qkv = jnp.moveaxis(grad[:, :, :3], 2, 0).reshape(3, rows, heads * HD)
        return qkv, grad[:, :, 3].transpose(1, 2, 0).reshape(heads * HD, rows)

    smalls = jnp.concatenate(
        [
            router_weight,
            attn_gain_one[:, None],
            first_feedforward_gain[:, None],
            attn_gain_two[:, None],
            moe_gain_two[:, None],
        ],
        axis=1,
    )
    smalls = jnp.pad(smalls, ((0, 0), (0, 128 - smalls.shape[1])))
    one = jnp.concatenate([attn_pack(qkv_weight_one, out_weight_one), smalls], axis=1)
    one = gather_planes(one)
    w_one = spread(one)
    mlp = jnp.stack([up_weight_one, down_weight_one.T])
    mlp = gather_planes(tie(mlp, one))
    w_mlp = spread(mlp)
    two = gather_planes(tie(attn_pack(qkv_weight_two, out_weight_two), mlp))

    def by_plane(experts):
        return [lax.dynamic_index_in_dim(experts, plane ^ m, 0, keepdims=False) for m in range(PLANES)]

    e_up = planes(tie(by_plane(expert_up), two))
    e_down = by_plane(jnp.swapaxes(expert_down, 1, 2))

    pad = ((0, padded - tokens), (0, 0))
    stream0 = jnp.pad(activations[0], pad)
    grad3 = jnp.pad(cotangent[0] * image_live[0].astype(f32), pad)
    routes = jnp.pad(expert_routes[0], pad, constant_values=-1)
    grad_low = grad3.astype(bf16)
    grad_half = jnp.where(core == 0, grad_low[:, :half], grad_low[:, half:])

    stream = shape((padded, model), f32)
    pieces = [shape((padded, half), f32), shape((padded, half), bf16)]
    wide = pltpu.VMEM((model, model + 128), held)
    square = pltpu.VMEM((model, model), held)
    unit = 2 * padded * model * model

    keep, send, small_rows = run(
        functools.partial(attn_fwd_kernel, tokens, parts, 4, True),
        scal,
        [stream0] + w_one,
        pieces + [shape((8, model), f32)],
        [wide],
        3 * unit,
    )
    own, other = joined(keep, send)
    own, other, two, e_up, e_down = bar(own, other, two, e_up, e_down)
    w_two, e_down = spread(two), planes(e_down)

    def stage_two(scal, *ins):
        stream1, keep, send = run(
            functools.partial(mlp_fwd_kernel, parts, 5),
            scal,
            ins,
            [stream] + pieces,
            [square, square],
            2 * unit,
        )
        return stream1, *joined(keep, send)

    stream1, own, other = enclosed(stage_two, scal, stream0, own, other, small_rows, *w_mlp)
    own, other, w_two, e_down, grad_half = bar(own, other, w_two, e_down, grad_half)
    w_e_up = spread(jnp.stack(e_up))
    g_near = planes([grad_half] * PLANES)[1:]

    def stage_three(scal, routes, small_rows, *ins):
        stream2, keep, send = run(
            functools.partial(attn_fwd_kernel, tokens, parts, 6, False),
            scal,
            [*ins[:3], small_rows, *ins[3:]],
            [stream] + pieces,
            [square],
            3 * unit,
        )
        outs = run(
            functools.partial(moe_pre_kernel, tokens, 7),
            scal,
            [stream2, *joined(keep, send), small_rows, routes],
            [stream, shape((padded, model), bf16), shape((padded, half), bf16)],
            [],
            unit / 50,
        )
        return stream2, *outs

    stream2, stream3, h_full, h_half = enclosed(
        stage_three, scal, routes, small_rows, stream1, own, other, *w_two
    )
    h_half, w_e_up, g_near = bar(h_half, w_e_up, g_near)
    h_near = planes([h_half] * PLANES)[1:]
    w_moe = w_e_up + spread(jnp.stack(e_down))
    h_blocks = [h_full] + h_near + [over(n, 1) for n in h_near]
    g_blocks = [grad_low] + g_near + [over(n, 1) for n in g_near]
    images = pltpu.VMEM((PLANES, padded, model), bf16)
    image_hidden = pltpu.VMEM((PLANES, padded, hidden), bf16)
    block_pieces = [shape((PLANES, padded, half), f32), shape((PLANES, padded, half), bf16)]
    y_keep, y_send, d_keep, d_send, *expert_grads = run(
        functools.partial(moe_kernel, parts),
        scal,
        h_blocks + g_blocks + w_moe,
        block_pieces * 2 + [shape((PLANES, rows, hidden), bf16)] * (2 * parts),
        [square, square, images, images, image_hidden, image_hidden, images, square],
        24 * unit,
        40,
    )

    def home(keep, send):
        summed = keep + over(send, 1).astype(f32)
        return planes(list(summed))

    block_grads = [shape((PLANES, rows, model), bf16)] * parts
    own, other = pair(added(home(d_keep, d_send)))
    e_up, e_down = fold(expert_grads[:parts]), fold_start(expert_grads[parts:])
    own, other, e_up = bar(own, other, e_up)
    e_up = planes(list(e_up))
    grad2, small, keep, send, *two_sum = run(
        functools.partial(attn_bwd_kernel, tokens, parts, (7, 6), False),
        scal,
        [stream3, own, other, grad3, small_rows, routes, stream2] + w_two,
        [stream, shape((8, model), f32)] + pieces + block_grads,
        [square, square],
        8 * unit,
    )
    keep, send, e_up, e_down = bar(keep, send, e_up, e_down)
    e_down = planes(list(added(e_down)))
    two_sum = fold(two_sum)
    own, other = joined(keep, send)
    own, other, e_down, two_sum = bar(own, other, e_down, two_sum)
    grad1, small, keep, send, *mlp_sum = run(
        functools.partial(mlp_bwd_kernel, parts, (6, 5)),
        scal,
        [stream2, own, other, grad2, small_rows, small, stream1] + w_mlp,
        [stream, shape((8, model), f32)]
        + pieces
        + [shape((PLANES, 2, rows, hidden), bf16)] * parts,
        [square, square, square],
        5 * unit,
    )
    mlp_sum = fold(mlp_sum)
    two_sum = planes(list(two_sum))
    own, other = joined(keep, send)
    y_keep, y_send = bar(y_keep, y_send, keep)[:2]
    y_own = home(y_keep, y_send)
    own, other, mlp_sum, two_sum, y_own = bar(own, other, mlp_sum, two_sum, y_own)
    mlp_sum = planes(list(mlp_sum))
    y_own, y_other = pair(added(y_own))
    grad0, small, keep, send, *one_sum = run(
        functools.partial(attn_bwd_kernel, tokens, parts, (5, 4), True),
        scal,
        [stream1, own, other, grad1, small_rows, small, stream0] + w_one,
        [stream, shape((8, model), f32)] + pieces + block_grads,
        [wide, square],
        8 * unit,
    )
    keep, send, mlp_sum[1] = bar(keep, send, mlp_sum[1])
    one_sum = fold(one_sum)
    own, other = joined(keep, send)
    one_sum = planes(list(one_sum))
    own, other, one_sum[1], mlp_sum = bar(own, other, one_sum[1], mlp_sum)
    input_grad, *small_grads = run(
        functools.partial(final_kernel, tokens, 4),
        scal,
        [stream0, own, other, grad0, small_rows, small],
        [shape((tokens, model), f32)] + [shape((PLANES, rows, 128), bf16)] * parts,
        [pltpu.VMEM((model, 128), f32)],
        unit / 50,
    )
    small_sum = reduce_planes(fold(small_grads))
    one_sum, two_sum, mlp_sum = added(one_sum), added(two_sum), added(mlp_sum)

    low = jnp.where(core == 0, y_own, y_other)
    high = jnp.where(core == 0, y_other, y_own)
    result = (stream3 + jnp.concatenate([low, high], axis=1).astype(f32))[:tokens]

    bit0, bit1 = plane % 2 == 1, plane // 2 == 1

    def of_expert(came, x):
        a, b = jnp.where(bit0, came[x ^ 1], came[x]), jnp.where(bit0, came[x ^ 3], came[x ^ 2])
        return jnp.where(bit1, b, a).astype(f32)

    grad_up = jnp.stack([of_expert(e_up, x) for x in range(PLANES)])
    grad_down = jnp.stack([of_expert(e_down, x).T for x in range(PLANES)])
    qkv_one, out_one = attn_unpack(one_sum)
    qkv_two, out_two = attn_unpack(two_sum)
    return (
        result[None],
        input_grad[None],
        small_sum[:, 4],
        qkv_one,
        out_one,
        small_sum[:, 5],
        mlp_sum[0],
        mlp_sum[1].T,
        small_sum[:, 6],
        qkv_two,
        out_two,
        small_sum[:, 7],
        small_sum[:, :PLANES],
        grad_up,
        grad_down,
    )


def solution(mesh):
    return jax.shard_map(
        functools.partial(shards, mesh.shape["fsdp"], mesh.shape["tensor"]),
        mesh=mesh,
        in_specs=(
            P("fsdp", None, None),
            P("fsdp"),
            P("fsdp", None, None),
            P("fsdp"),
            P(None, "fsdp", "tensor"),
            P("tensor", "fsdp"),
            P("fsdp"),
            P("fsdp", "tensor"),
            P("tensor", "fsdp"),
            P("fsdp"),
            P(None, "fsdp", "tensor"),
            P("tensor", "fsdp"),
            P("fsdp"),
            P("fsdp", None),
            P(None, "fsdp", "tensor"),
            P(None, "tensor", "fsdp"),
            P("fsdp", None, None),
        ),
        out_specs=(
            P("fsdp", None, None),
            P("fsdp", None, None),
            P("fsdp"),
            P(None, "fsdp", "tensor"),
            P("tensor", "fsdp"),
            P("fsdp"),
            P("fsdp", "tensor"),
            P("tensor", "fsdp"),
            P("fsdp"),
            P(None, "fsdp", "tensor"),
            P("tensor", "fsdp"),
            P("fsdp"),
            P("fsdp", None),
            P(None, "fsdp", "tensor"),
            P(None, "tensor", "fsdp"),
        ),
        check_vma=False,
    )
```
